256 devices in a mesh: replica: 32 (over z, y_lo, core), tp: 8 (over x, y_hi).
Axes of the slice: x: 4, y: 4 (y_hi: 2, y_lo: 2; y = y_hi * 2 + y_lo), z: 8, core: 2. Of those that a mesh axis runs over, the one named last changes fastest.
Arguments:
- hidden_in: bfloat16 [2, 256, 8192], P(None, 'replica'), may hold values from -1.796875 to 1.796875
- queries: bfloat16 [2, 256, 4096], P(None, 'replica', 'tp'), may hold values from -240 to 240
- new_keys: bfloat16 [2, 256, 1024], P(None, 'replica', 'tp'), may hold values from -6 to 6
- new_values: bfloat16 [2, 256, 1024], P(None, 'replica', 'tp'), may hold values from -6 to 6
- key_pool: bfloat16 [8, 1024, 128, 128], P('tp', 'replica'), may hold values from -6 to 6
- value_pool: bfloat16 [8, 1024, 128, 128], P('tp', 'replica'), may hold values from -6 to 6
- out_weight: bfloat16 [4096, 8192], P('tp'), may hold values from -0.09375 to 0.09375
- gain: float32 [8192], P('tp'), may hold values from 0.1 to 1.9
- lengths: int32 [32, 8], P('replica'), may hold values from 1 to 512, 2304 in all within a row
- block_table: int32 [256, 4], P('replica'), may hold values from 0 to 31, as said below
- mig_ids: int32 [32, 4], P('replica'), may hold values from 0 to 7, as said below
- partner: int32 [32], P('replica'), may hold values from 0 to 31, as said below
Outputs:
- mixed: bfloat16 [2, 256, 8192], P(None, 'replica', 'tp')
- moved_keys: bfloat16 [8, 512, 128, 128], P('tp', 'replica')
- moved_values: bfloat16 [8, 512, 128, 128], P('tp', 'replica')
The draws below stay inside these ranges and needn't reach their ends.
Inputs may be any that keep to these rules, and one draw needn't show every extreme that they name: `block_table`: each instance's entries are a permutation of 0 to 31. `mig_ids`: the ids of one instance are distinct. partner[r] is r XOR c for one c of 1 to 31, the same for all instances.
All inputs are finite; a program needn't handle non-finite values.
Results may differ from the reference program's by a relative error of at most 0.0051.
Values may be sent and summed in bfloat16 or wider, within the bound.
No kernel may reach another device: no remote copies, remote signals or barrier semaphores. Data moves between devices by JAX's collectives and lax.ppermute only.
A program may use at most 64 MiB of HBM per device.

```python
import math
import jax
import jax.numpy as jnp
import numpy as np
from jax import lax

D = 8192
KVH = 8
HEAD = 128
QPK = 4
PAGE = 128
PPR = 4
ROWS = 8
MIG = 4
HQ = 32
POOL = 32
CTX = 512
BATCH = 256
N_REPLICA = 32


def draw_queries(key, part):
    key = jax.random.fold_in(key, 1)
    first = jax.random.fold_in(key, 0)
    shape = (2, N_REPLICA * ROWS, KVH * QPK * HEAD)
    base = jnp.clip(jax.random.normal(first, shape, jnp.float32), -6.0, 6.0)
    return base.astype(jnp.bfloat16)


def draw_block_table(key, part):
    key = jax.random.fold_in(key, 2)
    instance_keys = jax.random.split(key, N_REPLICA)
    orders = jax.vmap(lambda single: jax.random.permutation(single, ROWS * PPR))(instance_keys)
    return orders.reshape(N_REPLICA * ROWS, PPR).astype(jnp.int32)


def draw_mig_ids(key, part):
    key = jax.random.fold_in(key, 3)
    instance_keys = jax.random.split(key, N_REPLICA)
    orders = jax.vmap(lambda single: jax.random.permutation(single, ROWS))(instance_keys)
    return orders[:, :MIG].astype(jnp.int32)


def draw_partner(key, part):
    key = jax.random.fold_in(key, 4)
    offset = jax.random.randint(key, (), 1, N_REPLICA, dtype=jnp.int32)
    return jnp.bitwise_xor(jnp.arange(N_REPLICA, dtype=jnp.int32), offset)


def block_levels(key, dims, cuts, least, top_value):
    def one(dim, blocks):
        heights = jax.random.uniform(jax.random.fold_in(jax.random.fold_in(key, 6), dim), (blocks,), jnp.float32, least / len(cuts), top_value / len(cuts))
        return jnp.repeat(jnp.exp(heights), dims[dim] // blocks).reshape((-1,) + (1,) * (len(dims) - dim - 1))

    loudness = one(*cuts[0])
    for cut in cuts[1:]:
        loudness = loudness * one(*cut)
    return loudness


def length_profile(amount, total, most, lean):
    portions = [(1 << 20) // math.isqrt(standing ** lean) + 1 for standing in range(2, amount + 1)]
    surplus, given = total - most - (amount - 1), [1] * (amount - 1)
    while surplus > 0:
        movable = [i for i in range(amount - 1) if given[i] < most]
        whole, budget = sum([portions[i] for i in movable]), surplus
        for i in movable:
            extra = min(most - given[i], max(1, budget * portions[i] // whole), surplus)
            given[i] = given[i] + extra
            surplus = surplus - extra
    return np.array([most] + given)


def ragged(key, count, total, bound, slope):
    if count == 2:
        one = jax.random.randint(key, (), max(1, total - bound), min(bound, total - 1) + 1)
        return jnp.stack([one, total - one])
    tallies = jnp.asarray(length_profile(count, total, bound, slope), jnp.int32)
    twos = (count - 1) // 2
    source_of, taker = tallies[1:1 + 2 * twos:2], tallies[2:2 + 2 * twos:2]
    slack = jnp.minimum(source_of - 1, bound - taker)
    passed = jax.random.randint(jax.random.fold_in(key, 1), (twos,), 0, 1 << 20) % (slack + 1)
    tallies = tallies.at[1:1 + 2 * twos:2].set(source_of - passed).at[2:2 + 2 * twos:2].set(taker + passed)
    return tallies[jax.random.permutation(jax.random.fold_in(key, 2), count)]


def gaussian(stream_key, dims, deviation, limit, shards=(), kind=jnp.bfloat16):
    array = jax.random.normal(stream_key, dims, jnp.float32) * deviation
    if len(shards) > 0:
        array = block_levels(stream_key, dims, shards, -0.22, 0.18) * array
    return jnp.clip(array, min=-limit, max=limit).astype(kind)


def setup_inputs(seed: int = 0) -> dict:
    streams_of = jax.random.split(jax.random.key(seed), 13)
    return {
        "hidden_in": gaussian(streams_of[0], (2, BATCH, D), 0.3, 1.796875, ((1, 32),)),
        "queries": draw_queries(jax.random.fold_in(streams_of[12], 71), 0),
        "new_keys": gaussian(streams_of[2], (2, BATCH, KVH * HEAD), 1.0, 6.0, ((1, 32), (2, 8))),
        "new_values": gaussian(streams_of[3], (2, BATCH, KVH * HEAD), 1.0, 6.0, ((1, 32), (2, 8))),
        "key_pool": gaussian(streams_of[4], (KVH, N_REPLICA * POOL, PAGE, HEAD), 1.0, 6.0, ((0, 8), (1, 32))),
        "value_pool": gaussian(streams_of[5], (KVH, N_REPLICA * POOL, PAGE, HEAD), 1.0, 6.0, ((0, 8), (1, 32))),
        "out_weight": gaussian(streams_of[6], (HQ * HEAD, D), (HQ * HEAD) ** -0.5, 0.09375, ((0, 8),)),
        "gain": jnp.clip(1.0 + 0.18 * jax.random.normal(streams_of[7], (D,), jnp.float32), 0.1, 1.9),
        "lengths": jax.vmap(lambda own: ragged(own, ROWS, CTX + (ROWS - 1) * CTX // 2, CTX, 2))(jax.random.split(streams_of[8], N_REPLICA)).reshape((N_REPLICA, ROWS)).astype(jnp.int32),
        "block_table": draw_block_table(jax.random.fold_in(streams_of[12], 71), 0),
        "mig_ids": draw_mig_ids(jax.random.fold_in(streams_of[12], 71), 0),
        "partner": draw_partner(jax.random.fold_in(streams_of[12], 71), 0),
    }


def attend(query_all, fresh_keys, fresh_values, key_pages, value_pages, page_table, row_lengths):
    step_count, row_count = (query_all.shape[0], query_all.shape[1])
    groups, head_size = (key_pages.shape[0], key_pages.shape[3])
    per_group = query_all.shape[2] // (groups * head_size)
    query_heads = query_all.reshape(step_count, row_count, groups, per_group, head_size).astype(jnp.float32)
    cached_keys = key_pages[:, page_table].reshape(groups, row_count, -1, head_size).astype(jnp.float32)
    cached_values = value_pages[:, page_table].reshape(groups, row_count, -1, head_size).astype(jnp.float32)
    new_k = fresh_keys.reshape(step_count, row_count, groups, head_size).astype(jnp.float32)
    new_v = fresh_values.reshape(step_count, row_count, groups, head_size).astype(jnp.float32)
    score_scale = 1.0 / jnp.sqrt(jnp.float32(head_size))
    cached = jnp.einsum('sbgje,gbte->sbgjt', query_heads, cached_keys) * score_scale
    context = cached_keys.shape[2]
    inside = jnp.arange(context, dtype=jnp.int32)[None, :] < row_lengths[:, None]
    cached = jnp.where(inside[None, :, None, None, :], cached, -jnp.inf)
    fresh = jnp.einsum('sbgje,tbge->sbgjt', query_heads, new_k) * score_scale
    causal = jnp.arange(step_count)[None, :] <= jnp.arange(step_count)[:, None]
    fresh = jnp.where(causal[:, None, None, None, :], fresh, -jnp.inf)
    largest = jnp.maximum(lax.optimization_barrier(jnp.max(cached, axis=-1)), lax.optimization_barrier(jnp.max(fresh, axis=-1)))[..., None]
    cached_exp = jnp.exp(cached - largest)
    fresh_exp = jnp.exp(fresh - largest)
    denominator = lax.optimization_barrier(jnp.sum(cached_exp, axis=-1, keepdims=True)) + lax.optimization_barrier(jnp.sum(fresh_exp, axis=-1, keepdims=True))
    cached_weights = (cached_exp / denominator).astype(jnp.bfloat16).astype(jnp.float32)
    fresh_weights = (fresh_exp / denominator).astype(jnp.bfloat16).astype(jnp.float32)
    result = jnp.einsum('sbgjt,gbte->sbgje', cached_weights, cached_values)
    result = result + jnp.einsum('sbgjt,tbge->sbgje', fresh_weights, new_v)
    return result.astype(jnp.bfloat16).reshape(step_count, row_count, groups * per_group * head_size)

def reference(hidden_in, queries, new_keys, new_values, key_pool, value_pool, out_weight, gain, lengths, block_table, mig_ids, partner):

    def per_instance(instance):
        start = instance * ROWS
        return attend(lax.dynamic_slice_in_dim(queries, start, ROWS, 1), lax.dynamic_slice_in_dim(new_keys, start, ROWS, 1), lax.dynamic_slice_in_dim(new_values, start, ROWS, 1), lax.dynamic_slice_in_dim(key_pool, instance * POOL, POOL, 1), lax.dynamic_slice_in_dim(value_pool, instance * POOL, POOL, 1), lax.dynamic_slice_in_dim(block_table, start, ROWS, 0), lax.dynamic_index_in_dim(lengths, instance, 0, keepdims=False))
    attn = lax.map(per_instance, jnp.arange(N_REPLICA, dtype=jnp.int32))
    attn = jnp.moveaxis(attn, 0, 1).reshape(2 * BATCH, HQ * HEAD)
    projected = jnp.dot(attn, out_weight, preferred_element_type=jnp.float32).reshape(2, BATCH, D)
    summed = hidden_in.astype(jnp.float32) + projected
    mean_square = lax.optimization_barrier(jnp.mean(summed * summed, axis=-1, keepdims=True))
    mixed = (summed * lax.rsqrt(mean_square + 1e-05) * gain).astype(jnp.bfloat16)
    instances = jnp.arange(N_REPLICA, dtype=jnp.int32)
    global_rows = mig_ids + (instances * ROWS)[:, None]
    page_ids = block_table[global_rows] + (instances * POOL)[:, None, None]
    source_pages = page_ids[partner].reshape(-1)
    return (mixed, key_pool[:, source_pages], value_pool[:, source_pages])
```

```python
import functools

import jax
import jax.numpy as jnp
from jax import lax
from jax.experimental import pallas as pl
from jax.experimental.pallas import tpu as pltpu
from jax.sharding import PartitionSpec as P

VMEM = pl.BlockSpec(memory_space=pltpu.VMEM)
SMEM = pl.BlockSpec(memory_space=pltpu.SMEM)
HBM = pl.BlockSpec(memory_space=pl.ANY)


def gather_kernel(table, ids, keys, values, keys_out, values_out, sems):
    count, pages = (ids.shape[1], table.shape[1])
    copies = []
    for pool, out in ((keys, keys_out), (values, values_out)):
        for m in range(count):
            for i in range(pages):
                copy = pltpu.make_async_copy(
                    pool.at[:, pl.ds(table[ids[0, m], i], 1)],
                    out.at[:, pl.ds(m * pages + i, 1)],
                    sems.at[len(copies)],
                )
                copy.start()
                copies.append(copy)
    for copy in copies:
        copy.wait()


def gather_pages(block_table, mig_ids, key_pool, value_pool):
    moved = mig_ids.shape[1] * block_table.shape[1]
    shape = jax.ShapeDtypeStruct((1, moved) + key_pool.shape[2:], key_pool.dtype)
    return pl.pallas_call(
        gather_kernel,
        out_shape=(shape, shape),
        in_specs=[SMEM, SMEM, HBM, HBM],
        out_specs=(HBM, HBM),
        scratch_shapes=[pltpu.SemaphoreType.DMA((2 * moved,))],
        cost_estimate=pl.CostEstimate(flops=0, bytes_accessed=1 << 22, transcendentals=0),
    )(block_table, mig_ids, key_pool, value_pool)


def attend_kernel(
    table, lengths, queries, new_keys, new_values, keys, values, weight,
    out, key_buf, value_buf, weight_buf, query_rows, attn_rows, sems,
):
    steps, rows, width = queries.shape
    page, head = key_buf.shape[1:]
    per_group = width // head
    pages = table.shape[1]
    parts, columns = (weight_buf.shape[0], weight_buf.shape[2])

    def weight_copy(t):
        start = pl.multiple_of(t * columns, columns)
        return pltpu.make_async_copy(
            weight.at[:, pl.ds(start, columns)], weight_buf.at[t], sems.at[2 + t]
        )

    key_copy = pltpu.make_async_copy(keys.at[0], key_buf, sems.at[0])
    value_copy = pltpu.make_async_copy(values.at[0], value_buf, sems.at[1])
    key_copy.start()
    value_copy.start()
    for t in range(parts):
        weight_copy(t).start()

    for s in range(steps):
        both = queries[s].astype(jnp.float32)
        for j in range(per_group):
            query_rows[:, s * per_group + j, :] = both[:, j * head : (j + 1) * head]
    fresh_k = [new_keys[s].astype(jnp.float32) for s in range(steps)]
    fresh_v = [new_values[s].astype(jnp.float32) for s in range(steps)]
    scale = 1.0 / jnp.sqrt(jnp.float32(head))
    count = steps * per_group
    step_of = lax.broadcasted_iota(jnp.int32, (count, 1), 0) // per_group
    position = lax.broadcasted_iota(jnp.int32, (count, pages * page), 1)

    key_copy.wait()
    weights, fresh_weights = ([], [])
    for b in range(rows):
        query = query_rows[b]
        cached_k = jnp.concatenate([key_buf[table[b, i]] for i in range(pages)], axis=0)
        scores = lax.dot_general(
            query.astype(jnp.bfloat16),
            cached_k,
            (((1,), (1,)), ((), ())),
            preferred_element_type=jnp.float32,
        )
        scores = jnp.where(position < lengths[0, b], scores * scale, -jnp.inf)
        largest = jnp.max(scores, axis=1, keepdims=True)
        fresh = []
        for s in range(steps):
            one = jnp.sum(query * fresh_k[s][b : b + 1], axis=1, keepdims=True) * scale
            one = jnp.where(step_of >= s, one, -jnp.inf)
            largest = jnp.maximum(largest, one)
            fresh.append(one)
        raised = jnp.exp(scores - largest)
        fresh = [jnp.exp(one - largest) for one in fresh]
        total = jnp.sum(raised, axis=1, keepdims=True)
        for one in fresh:
            total = total + one
        weights.append((raised / total).astype(jnp.bfloat16))
        fresh_weights.append([(one / total).astype(jnp.bfloat16).astype(jnp.float32) for one in fresh])

    value_copy.wait()
    for b in range(rows):
        cached_v = jnp.concatenate([value_buf[table[b, i]] for i in range(pages)], axis=0)
        result = jnp.dot(weights[b], cached_v, preferred_element_type=jnp.float32)
        for s in range(steps):
            result = result + fresh_weights[b][s] * fresh_v[s][b : b + 1]
        attn_rows[b] = result

    attn = jnp.concatenate(
        [
            jnp.concatenate([attn_rows[:, s * per_group + j, :] for j in range(per_group)], axis=1)
            for s in range(steps)
        ],
        axis=0,
    ).astype(jnp.bfloat16)

    def project(t, carry):
        weight_copy(t).wait()
        out[t] = jnp.dot(attn, weight_buf[t], preferred_element_type=jnp.float32).astype(out.dtype)
        return carry

    lax.fori_loop(0, parts, project, 0)


def attend_project(
    block_table, lengths, queries, new_keys, new_values, key_pool, value_pool, out_weight, parts
):
    steps, rows, width = queries.shape
    pool, page, head = key_pool.shape[1:]
    columns = out_weight.shape[1] // parts
    heads = width // head
    return pl.pallas_call(
        attend_kernel,
        out_shape=jax.ShapeDtypeStruct((parts, steps * rows, columns), jnp.float32),
        in_specs=[SMEM, SMEM, VMEM, VMEM, VMEM, HBM, HBM, HBM],
        out_specs=VMEM,
        scratch_shapes=[
            pltpu.VMEM((pool, page, head), key_pool.dtype),
            pltpu.VMEM((pool, page, head), value_pool.dtype),
            pltpu.VMEM((parts, width, columns), out_weight.dtype),
            pltpu.VMEM((rows, steps * heads, head), jnp.float32),
            pltpu.VMEM((rows, steps * heads, head), jnp.float32),
            pltpu.SemaphoreType.DMA((2 + parts,)),
        ],
        compiler_params=pltpu.CompilerParams(vmem_limit_bytes=24 << 20),
        cost_estimate=pl.CostEstimate(
            flops=160_000_000, bytes_accessed=11 << 20, transcendentals=32768
        ),
    )(block_table, lengths, queries, new_keys, new_values, key_pool, value_pool, out_weight)


def sum_kernel(parts, residual, summed, squares):
    total = parts[0]
    for t in range(1, parts.shape[0]):
        total = total + parts[t]
    rows = jnp.concatenate([residual[s].astype(jnp.float32) for s in range(residual.shape[0])], axis=0)
    total = total + rows
    summed[...] = total
    square = jnp.sum(total * total, axis=1, keepdims=True)
    square = jnp.broadcast_to(square, squares.shape[1:])
    for t in range(squares.shape[0]):
        squares[t] = square


def add_parts(parts, residual):
    count, rows, columns = parts.shape
    return pl.pallas_call(
        sum_kernel,
        out_shape=(
            jax.ShapeDtypeStruct((rows, columns), jnp.float32),
            jax.ShapeDtypeStruct((count, rows, 128), jnp.float32),
        ),
        in_specs=[VMEM, VMEM],
        out_specs=(VMEM, VMEM),
        cost_estimate=pl.CostEstimate(flops=200_000, bytes_accessed=700_000, transcendentals=0),
    )(parts, residual)


def norm_kernel(features, squares, summed, gain, mixed):
    total = squares[0]
    for t in range(1, squares.shape[0]):
        total = total + squares[t]
    factor = lax.rsqrt(total[:, :1] / features + 1e-05)
    scaled = (summed[...] * factor * gain[...]).astype(mixed.dtype)
    rows = mixed.shape[1]
    for s in range(mixed.shape[0]):
        mixed[s] = scaled[s * rows : (s + 1) * rows]


def norm(squares, summed, gain, steps, features):
    rows, columns = summed.shape
    return pl.pallas_call(
        functools.partial(norm_kernel, features),
        out_shape=jax.ShapeDtypeStruct((steps, rows // steps, columns), jnp.bfloat16),
        in_specs=[VMEM, VMEM, VMEM],
        out_specs=VMEM,
        cost_estimate=pl.CostEstimate(flops=50_000, bytes_accessed=200_000, transcendentals=16),
    )(squares, summed, gain.reshape(1, columns))


def layer(
    hidden_in, queries, new_keys, new_values, key_pool, value_pool, out_weight, gain, lengths, block_table
):
    tp = lax.axis_size("tp")
    columns = gain.shape[0]
    partial_sums = attend_project(
        block_table, lengths, queries, new_keys, new_values, key_pool, value_pool, out_weight, tp
    )
    parts = lax.all_to_all(partial_sums, "tp", 0, 0, tiled=True)
    residual = lax.dynamic_slice_in_dim(hidden_in, lax.axis_index("tp") * columns, columns, 2)
    summed, squares = add_parts(parts, residual)
    squares = lax.all_to_all(squares, "tp", 0, 0, tiled=True)
    return norm(squares, summed, gain, hidden_in.shape[0], hidden_in.shape[2])


def shards(
    hidden_in,
    queries,
    new_keys,
    new_values,
    key_pool,
    value_pool,
    out_weight,
    gain,
    lengths,
    block_table,
    mig_ids,
    partner,
):
    count = lax.axis_size("replica")
    offset = jnp.bitwise_xor(partner[0], lax.axis_index("replica"))
    moving_keys, moving_values = gather_pages(block_table, mig_ids, key_pool, value_pool)

    def branch(distance):
        route = [(i, i ^ distance) for i in range(count)]

        def body(moving_keys, moving_values, *rest):
            moved_keys = lax.ppermute(moving_keys, "replica", route)
            moved_values = lax.ppermute(moving_values, "replica", route)
            return (layer(*rest), moved_keys, moved_values)

        return body

    return lax.switch(
        offset - 1,
        [branch(distance) for distance in range(1, count)],
        moving_keys,
        moving_values,
        hidden_in,
        queries,
        new_keys,
        new_values,
        key_pool,
        value_pool,
        out_weight,
        gain,
        lengths,
        block_table,
    )


def solution(mesh):
    placed = (
        P(None, "replica", None),
        P(None, "replica", "tp"),
        P(None, "replica", "tp"),
        P(None, "replica", "tp"),
        P("tp", "replica", None, None),
        P("tp", "replica", None, None),
        P("tp", None),
        P("tp"),
        P("replica", None),
        P("replica", None),
        P("replica", None),
        P("replica"),
    )
    return jax.shard_map(
        shards,
        mesh=mesh,
        in_specs=placed,
        out_specs=(
            P(None, "replica", "tp"),
            P("tp", "replica", None, None),
            P("tp", "replica", None, None),
        ),
        check_vma=False,
    )
```

```python
import functools

import jax
import jax.numpy as jnp
from jax import lax
from jax.experimental import pallas as pl
from jax.experimental.pallas import tpu as pltpu
from jax.sharding import PartitionSpec as P

CUT = 512
VMEM = pl.BlockSpec(memory_space=pltpu.VMEM)
SMEM = pl.BlockSpec(memory_space=pltpu.SMEM)
HBM = pl.BlockSpec(memory_space=pl.ANY)


def gather_kernel(table, ids, keys, values, out, sems):
    count, pages = (ids.shape[1], table.shape[0])
    copies = []
    for k, pool in enumerate((keys, values)):
        for m in range(count):
            for i in range(pages):
                copy = pltpu.make_async_copy(
                    pool.at[:, pl.ds(table[i, ids[0, m]], 1)],
                    out.at[pl.ds(k, 1), pl.ds(m * pages + i, 1)],
                    sems.at[len(copies)],
                )
                copy.start()
                copies.append(copy)
    for copy in copies:
        copy.wait()


def gather_pages(block_table, mig_ids, key_pool, value_pool):
    moved = mig_ids.shape[1] * block_table.shape[0]
    shape = jax.ShapeDtypeStruct((2, moved) + key_pool.shape[2:], key_pool.dtype)
    return pl.pallas_call(
        gather_kernel,
        out_shape=shape,
        in_specs=[SMEM, SMEM, HBM, HBM],
        out_specs=HBM,
        scratch_shapes=[pltpu.SemaphoreType.DMA((2 * moved,))],
        cost_estimate=pl.CostEstimate(flops=0, bytes_accessed=1 << 22, transcendentals=0),
    )(block_table, mig_ids, key_pool, value_pool)


def attend_kernel(
    table, lengths, queries, new_keys, new_values, keys, values, weight,
    out, key_buf, value_buf, weight_buf, query_rows, attn_rows, fresh_k, fresh_v, sems,
):
    steps, rows, width = queries.shape
    page, head = key_buf.shape[1:]
    per_group = width // head
    pages = table.shape[0]
    parts, columns = (weight_buf.shape[0], weight_buf.shape[2])

    def weight_copy(t):
        start = pl.multiple_of(t * columns, columns)
        return pltpu.make_async_copy(
            weight.at[:, pl.ds(start, columns)], weight_buf.at[t], sems.at[2 + t]
        )

    key_copy = pltpu.make_async_copy(keys.at[0], key_buf, sems.at[0])
    value_copy = pltpu.make_async_copy(values.at[0], value_buf, sems.at[1])
    key_copy.start()
    value_copy.start()
    def start_weight(t, carry):
        weight_copy(t).start()
        return carry

    lax.fori_loop(0, parts, start_weight, 0)

    for s in range(steps):
        both = queries[s].astype(jnp.float32)
        for j in range(per_group):
            query_rows[:, s * per_group + j, :] = both[:, j * head : (j + 1) * head]
        fresh_k[s] = new_keys[s].astype(jnp.float32)
        fresh_v[s] = new_values[s].astype(jnp.float32)
    scale = 1.0 / jnp.sqrt(jnp.float32(head))
    count = steps * per_group
    step_of = lax.broadcasted_iota(jnp.int32, (count, 1), 0) // per_group
    position = lax.broadcasted_iota(jnp.int32, (count, pages * page), 1)

    key_copy.wait()
    value_copy.wait()

    def attend_row(b, carry):
        query = query_rows[b]
        cached_k = jnp.concatenate([key_buf[table[i, b]] for i in range(pages)], axis=0)
        scores = lax.dot_general(
            query.astype(jnp.bfloat16),
            cached_k,
            (((1,), (1,)), ((), ())),
            preferred_element_type=jnp.float32,
        )
        scores = jnp.where(position < lengths[0, b], scores * scale, -jnp.inf)
        largest = jnp.max(scores, axis=1, keepdims=True)
        fresh = []
        for s in range(steps):
            one = jnp.sum(query * fresh_k[s, pl.ds(b, 1)], axis=1, keepdims=True) * scale
            one = jnp.where(step_of >= s, one, -jnp.inf)
            largest = jnp.maximum(largest, one)
            fresh.append(one)
        raised = jnp.exp(scores - largest)
        fresh = [jnp.exp(one - largest) for one in fresh]
        total = jnp.sum(raised, axis=1, keepdims=True)
        for one in fresh:
            total = total + one
        cached_v = jnp.concatenate([value_buf[table[i, b]] for i in range(pages)], axis=0)
        result = jnp.dot(
            (raised / total).astype(jnp.bfloat16), cached_v, preferred_element_type=jnp.float32
        )
        for s in range(steps):
            weight = (fresh[s] / total).astype(jnp.bfloat16).astype(jnp.float32)
            result = result + weight * fresh_v[s, pl.ds(b, 1)]
        attn_rows[b] = result
        return carry

    lax.fori_loop(0, rows, attend_row, 0, unroll=1)

    attn = jnp.concatenate(
        [
            jnp.concatenate([attn_rows[:, s * per_group + j, :] for j in range(per_group)], axis=1)
            for s in range(steps)
        ],
        axis=0,
    ).astype(jnp.bfloat16)

    def project(t, carry):
        weight_copy(t).wait()

        def piece(u, inner):
            at = pl.ds(pl.multiple_of(u * CUT, CUT), CUT)
            product = jnp.dot(attn, weight_buf[t, :, at], preferred_element_type=jnp.float32)
            out[t, :, at] = product.astype(out.dtype)
            return inner

        return lax.fori_loop(0, columns // CUT, piece, carry)

    lax.fori_loop(0, parts, project, 0)


def attend_project(
    block_table, lengths, queries, new_keys, new_values, key_pool, value_pool, out_weight, parts
):
    steps, rows, width = queries.shape
    pool, page, head = key_pool.shape[1:]
    columns = out_weight.shape[1] // parts
    heads = width // head
    return pl.pallas_call(
        attend_kernel,
        out_shape=jax.ShapeDtypeStruct((parts, steps * rows, columns), jnp.bfloat16),
        in_specs=[SMEM, SMEM, VMEM, VMEM, VMEM, HBM, HBM, HBM],
        out_specs=VMEM,
        scratch_shapes=[
            pltpu.VMEM((pool, page, head), key_pool.dtype),
            pltpu.VMEM((pool, page, head), value_pool.dtype),
            pltpu.VMEM((parts, width, columns), out_weight.dtype),
            pltpu.VMEM((rows, steps * heads, head), jnp.float32),
            pltpu.VMEM((rows, steps * heads, head), jnp.float32),
            pltpu.VMEM((steps, rows, head), jnp.float32),
            pltpu.VMEM((steps, rows, head), jnp.float32),
            pltpu.SemaphoreType.DMA((2 + parts,)),
        ],
        compiler_params=pltpu.CompilerParams(vmem_limit_bytes=24 << 20),
        cost_estimate=pl.CostEstimate(
            flops=160_000_000, bytes_accessed=11 << 20, transcendentals=32768
        ),
    )(block_table, lengths, queries, new_keys, new_values, key_pool, value_pool, out_weight)


def sum_kernel(parts, residual, summed, squares):
    total = parts[0].astype(jnp.float32)
    for t in range(1, parts.shape[0]):
        total = total + parts[t].astype(jnp.float32)
    rows = jnp.concatenate([residual[s].astype(jnp.float32) for s in range(residual.shape[0])], axis=0)
    total = total + rows
    summed[...] = total
    square = jnp.sum(total * total, axis=1, keepdims=True)
    square = jnp.broadcast_to(square, squares.shape[1:])
    for t in range(squares.shape[0]):
        squares[t] = square


def add_parts(parts, residual):
    count, rows, columns = parts.shape
    return pl.pallas_call(
        sum_kernel,
        out_shape=(
            jax.ShapeDtypeStruct((rows, columns), jnp.float32),
            jax.ShapeDtypeStruct((count, rows, 128), jnp.float32),
        ),
        in_specs=[VMEM, VMEM],
        out_specs=(VMEM, VMEM),
        cost_estimate=pl.CostEstimate(flops=200_000, bytes_accessed=700_000, transcendentals=0),
    )(parts, residual)


def finish_kernel(
    features, squares, summed, gain, moved, mixed, keys_out, values_out, buf, in_sems, out_sems
):
    pieces, size = (in_sems.shape[0], buf.shape[1] * buf.shape[0] // in_sems.shape[0])
    per_array = pieces // 2

    def at(k):
        return (pl.ds(k // per_array, 1), pl.ds(k % per_array * size, size))

    arrive = [
        pltpu.make_async_copy(moved.at[at(k)], buf.at[at(k)], in_sems.at[k]) for k in range(pieces)
    ]
    leave = [
        pltpu.make_async_copy(
            buf.at[at(k)],
            (keys_out, values_out)[k // per_array].at[:, pl.ds(k % per_array * size, size)],
            out_sems.at[k],
        )
        for k in range(pieces)
    ]
    for copy in arrive:
        copy.start()
    for k in range(pieces):
        arrive[k].wait()
        leave[k].start()
    total = squares[0]
    for t in range(1, squares.shape[0]):
        total = total + squares[t]
    factor = lax.rsqrt(total[:, :1] / features + 1e-05)
    scaled = (summed[...] * factor * gain[...]).astype(mixed.dtype)
    rows = mixed.shape[1]
    for s in range(mixed.shape[0]):
        mixed[s] = scaled[s * rows : (s + 1) * rows]
    for copy in leave:
        copy.wait()


def finish(squares, summed, gain, moved, steps, features):
    rows, columns = summed.shape
    pieces = 4
    shape = jax.ShapeDtypeStruct((1,) + moved.shape[1:], moved.dtype)
    return pl.pallas_call(
        functools.partial(finish_kernel, features),
        out_shape=(
            jax.ShapeDtypeStruct((steps, rows // steps, columns), jnp.bfloat16),
            shape,
            shape,
        ),
        in_specs=[VMEM, VMEM, VMEM, HBM],
        out_specs=(VMEM, HBM, HBM),
        scratch_shapes=[
            pltpu.VMEM(moved.shape, moved.dtype),
            pltpu.SemaphoreType.DMA((pieces,)),
            pltpu.SemaphoreType.DMA((pieces,)),
        ],
        cost_estimate=pl.CostEstimate(flops=50_000, bytes_accessed=1 << 22, transcendentals=16),
    )(squares, summed, gain.reshape(1, columns), moved)


def layer(residual, *attended):
    partial_sums = attend_project(*attended, lax.axis_size("tp"))
    parts = lax.all_to_all(partial_sums, "tp", 0, 0, tiled=True)
    summed, squares = add_parts(parts, residual)
    return (lax.all_to_all(squares, "tp", 0, 0, tiled=True), summed)


def shards(
    hidden_in,
    queries,
    new_keys,
    new_values,
    key_pool,
    value_pool,
    out_weight,
    gain,
    lengths,
    block_table,
    mig_ids,
    partner,
):
    count = lax.axis_size("replica")
    offset = jnp.bitwise_xor(partner[0], lax.axis_index("replica"))
    page_table = block_table.T
    moving = gather_pages(page_table, mig_ids, key_pool, value_pool)
    residual = lax.dynamic_slice_in_dim(
        hidden_in, lax.axis_index("tp") * gain.shape[0], gain.shape[0], 2
    )

    def branch(distance):
        route = [(i, i ^ distance) for i in range(count)]

        def body(moving, *rest):
            moved = lax.ppermute(moving, "replica", route)
            return (*layer(*rest), moved)

        return body

    squares, summed, moved = lax.switch(
        offset - 1,
        [branch(distance) for distance in range(1, count)],
        moving, residual,
        page_table, lengths, queries, new_keys, new_values, key_pool, value_pool, out_weight,
    )
    return finish(squares, summed, gain, moved, hidden_in.shape[0], hidden_in.shape[2])


def solution(mesh):
    placed = (
        P(None, "replica", None),
        P(None, "replica", "tp"),
        P(None, "replica", "tp"),
        P(None, "replica", "tp"),
        P("tp", "replica", None, None),
        P("tp", "replica", None, None),
        P("tp", None),
        P("tp"),
        P("replica", None),
        P("replica", None),
        P("replica", None),
        P("replica"),
    )
    return jax.shard_map(
        shards,
        mesh=mesh,
        in_specs=placed,
        out_specs=(
            P(None, "replica", "tp"),
            P("tp", "replica", None, None),
            P("tp", "replica", None, None),
        ),
        check_vma=False,
    )
```

```python
import functools

import jax
import jax.numpy as jnp
from jax import lax
from jax.experimental import pallas as pl
from jax.experimental.pallas import tpu as pltpu
from jax.sharding import PartitionSpec as P

CUT = 512
VMEM = pl.BlockSpec(memory_space=pltpu.VMEM)
SMEM = pl.BlockSpec(memory_space=pltpu.SMEM)
ANY = pl.BlockSpec(memory_space=pl.ANY)
HBM = pl.BlockSpec(memory_space=pltpu.HBM)


def gather_kernel(
    table_in, ids_in, keys, values, hidden, out, residual, table, ids, scalar_sems, sems, row_sem
):
    count, pages = (ids.shape[1], table.shape[0])
    scalars = [
        pltpu.make_async_copy(table_in, table, scalar_sems.at[0]),
        pltpu.make_async_copy(ids_in, ids, scalar_sems.at[1]),
    ]
    columns = residual.shape[1]
    own = pl.ds(pl.multiple_of(lax.axis_index("tp") * columns, columns), columns)
    rows = pltpu.make_async_copy(hidden.at[:, own], residual, row_sem)
    for copy in scalars:
        copy.start()
    rows.start()
    for copy in scalars:
        copy.wait()
    for m in range(count):
        row = ids[0, m]
        for i in range(pages):
            source = pl.ds(table[i, row], 1)
            target = pl.ds(m * pages + i, 1)
            for k, pool in enumerate((keys, values)):
                pltpu.make_async_copy(
                    pool.at[:, source], out.at[pl.ds(k, 1), target], sems.at[k]
                ).start()
    for k, pool in enumerate((keys, values)):
        pltpu.make_async_copy(
            pool.at[:, pl.ds(0, count * pages)], out.at[pl.ds(k, 1)], sems.at[k]
        ).wait()
    rows.wait()


def gather_pages(block_table, mig_ids, key_pool, value_pool, hidden, columns):
    moved = mig_ids.shape[1] * block_table.shape[0]
    shape = jax.ShapeDtypeStruct((2, moved) + key_pool.shape[2:], key_pool.dtype)
    return pl.pallas_call(
        gather_kernel,
        out_shape=(shape, jax.ShapeDtypeStruct((hidden.shape[0], columns), hidden.dtype)),
        in_specs=[HBM, HBM, ANY, ANY, ANY],
        out_specs=(ANY, ANY),
        scratch_shapes=[
            pltpu.SMEM(block_table.shape, block_table.dtype),
            pltpu.SMEM(mig_ids.shape, mig_ids.dtype),
            pltpu.SemaphoreType.DMA((2,)),
            pltpu.SemaphoreType.DMA((2,)),
            pltpu.SemaphoreType.DMA,
        ],
        cost_estimate=pl.CostEstimate(flops=0, bytes_accessed=1 << 22, transcendentals=0),
    )(block_table, mig_ids, key_pool, value_pool, hidden)


def attend_kernel(
    table, lengths, queries, new_keys, new_values, keys, values, weight,
    out, key_buf, value_buf, weight_buf, query_rows, attn_rows, fresh_k, fresh_v, sems,
):
    steps, rows, width = queries.shape
    page, head = key_buf.shape[1:]
    per_group = width // head
    pages = table.shape[0]
    parts, columns = (weight_buf.shape[0], weight_buf.shape[2])

    def weight_copy(t):
        start = pl.multiple_of(t * columns, columns)
        return pltpu.make_async_copy(
            weight.at[:, pl.ds(start, columns)], weight_buf.at[t], sems.at[2 + t]
        )

    key_copy = pltpu.make_async_copy(keys.at[0], key_buf, sems.at[0])
    value_copy = pltpu.make_async_copy(values.at[0], value_buf, sems.at[1])
    key_copy.start()
    value_copy.start()
    def start_weight(t, carry):
        weight_copy(t).start()
        return carry

    lax.fori_loop(0, parts, start_weight, 0)

    for s in range(steps):
        both = queries[s].astype(jnp.float32)
        for j in range(per_group):
            query_rows[:, s * per_group + j, :] = both[:, j * head : (j + 1) * head]
        fresh_k[s] = new_keys[s].astype(jnp.float32)
        fresh_v[s] = new_values[s].astype(jnp.float32)
    scale = 1.0 / jnp.sqrt(jnp.float32(head))
    count = steps * per_group
    step_of = lax.broadcasted_iota(jnp.int32, (count, 1), 0) // per_group
    position = lax.broadcasted_iota(jnp.int32, (count, pages * page), 1)

    key_copy.wait()
    value_copy.wait()

    def attend_row(b, carry):
        query = query_rows[b]
        cached_k = jnp.concatenate([key_buf[table[i, b]] for i in range(pages)], axis=0)
        scores = lax.dot_general(
            query.astype(jnp.bfloat16),
            cached_k,
            (((1,), (1,)), ((), ())),
            preferred_element_type=jnp.float32,
        )
        scores = jnp.where(position < lengths[0, b], scores * scale, -jnp.inf)
        largest = jnp.max(scores, axis=1, keepdims=True)
        fresh = []
        for s in range(steps):
            one = jnp.sum(query * fresh_k[s, pl.ds(b, 1)], axis=1, keepdims=True) * scale
            one = jnp.where(step_of >= s, one, -jnp.inf)
            largest = jnp.maximum(largest, one)
            fresh.append(one)
        raised = jnp.exp(scores - largest)
        fresh = [jnp.exp(one - largest) for one in fresh]
        total = jnp.sum(raised, axis=1, keepdims=True)
        for one in fresh:
            total = total + one
        cached_v = jnp.concatenate([value_buf[table[i, b]] for i in range(pages)], axis=0)
        result = jnp.dot(
            (raised / total).astype(jnp.bfloat16), cached_v, preferred_element_type=jnp.float32
        )
        for s in range(steps):
            weight = (fresh[s] / total).astype(jnp.bfloat16).astype(jnp.float32)
            result = result + weight * fresh_v[s, pl.ds(b, 1)]
        attn_rows[b] = result
        return carry

    lax.fori_loop(0, rows, attend_row, 0, unroll=1)

    attn = jnp.concatenate(
        [
            jnp.concatenate([attn_rows[:, s * per_group + j, :] for j in range(per_group)], axis=1)
            for s in range(steps)
        ],
        axis=0,
    ).astype(jnp.bfloat16)

    def project(t, carry):
        weight_copy(t).wait()

        def piece(u, inner):
            at = pl.ds(pl.multiple_of(u * CUT, CUT), CUT)
            product = jnp.dot(attn, weight_buf[t, :, at], preferred_element_type=jnp.float32)
            out[t, :, at] = product.astype(out.dtype)
            return inner

        return lax.fori_loop(0, columns // CUT, piece, carry)

    lax.fori_loop(0, parts, project, 0)


def attend_project(
    block_table, lengths, queries, new_keys, new_values, key_pool, value_pool, out_weight, parts
):
    steps, rows, width = queries.shape
    pool, page, head = key_pool.shape[1:]
    columns = out_weight.shape[1] // parts
    heads = width // head
    return pl.pallas_call(
        attend_kernel,
        out_shape=jax.ShapeDtypeStruct((parts, steps * rows, columns), jnp.bfloat16),
        in_specs=[SMEM, SMEM, VMEM, VMEM, VMEM, ANY, ANY, ANY],
        out_specs=VMEM,
        scratch_shapes=[
            pltpu.VMEM((pool, page, head), key_pool.dtype),
            pltpu.VMEM((pool, page, head), value_pool.dtype),
            pltpu.VMEM((parts, width, columns), out_weight.dtype),
            pltpu.VMEM((rows, steps * heads, head), jnp.float32),
            pltpu.VMEM((rows, steps * heads, head), jnp.float32),
            pltpu.VMEM((steps, rows, head), jnp.float32),
            pltpu.VMEM((steps, rows, head), jnp.float32),
            pltpu.SemaphoreType.DMA((2 + parts,)),
        ],
        compiler_params=pltpu.CompilerParams(vmem_limit_bytes=24 << 20),
        cost_estimate=pl.CostEstimate(
            flops=160_000_000, bytes_accessed=11 << 20, transcendentals=32768
        ),
    )(block_table, lengths, queries, new_keys, new_values, key_pool, value_pool, out_weight)


def diagonal(rows):
    at = [lax.broadcasted_iota(jnp.int32, (rows, 128), axis) for axis in range(2)]
    return at[0] == at[1]


def sum_kernel(parts, residual, summed, squares):
    total = parts[0].astype(jnp.float32)
    for t in range(1, parts.shape[0]):
        total = total + parts[t].astype(jnp.float32)
    total = total + residual[...].astype(jnp.float32)
    summed[...] = total
    square = jnp.sum(total * total, axis=1, keepdims=True)
    square = jnp.sum(jnp.where(diagonal(total.shape[0]), square, 0.0), axis=0, keepdims=True)
    for t in range(squares.shape[0]):
        squares[t] = square


def add_parts(parts, residual):
    count, rows, columns = parts.shape
    return pl.pallas_call(
        sum_kernel,
        out_shape=(
            jax.ShapeDtypeStruct((rows, columns), jnp.float32),
            jax.ShapeDtypeStruct((count, 1, 128), jnp.float32),
        ),
        in_specs=[VMEM, VMEM],
        out_specs=(VMEM, VMEM),
        cost_estimate=pl.CostEstimate(flops=200_000, bytes_accessed=700_000, transcendentals=0),
    )(parts, residual)


def finish_kernel(
    features, squares_in, summed_in, gain_in, moved, mixed_out, keys_out, values_out,
    squares, summed, gain, buf, mixed, in_sems, page_sems, out_sems,
):
    pieces = page_sems.shape[0]
    per_array = pieces // 2
    size = buf.shape[1] // per_array

    def at(k):
        return (pl.ds(k // per_array, 1), pl.ds(k % per_array * size, size))

    arrive = [
        pltpu.make_async_copy(moved.at[at(k)], buf.at[at(k)], page_sems.at[k]) for k in range(pieces)
    ]
    small = [
        pltpu.make_async_copy(source, target, in_sems.at[k])
        for k, (source, target) in enumerate(
            ((squares_in, squares), (summed_in, summed), (gain_in, gain))
        )
    ]
    leave = [
        pltpu.make_async_copy(
            buf.at[at(k)],
            (keys_out, values_out)[k // per_array].at[:, pl.ds(k % per_array * size, size)],
            out_sems.at[k],
        )
        for k in range(pieces)
    ]
    leave.append(pltpu.make_async_copy(mixed, mixed_out, out_sems.at[pieces]))
    for copy in arrive + small:
        copy.start()
    for k in range(pieces):
        arrive[k].wait()
        leave[k].start()
    for copy in small:
        copy.wait()
    total = squares[0]
    for t in range(1, squares.shape[0]):
        total = total + squares[t]
    total = jnp.where(diagonal(summed.shape[0]), total, 0.0)
    factor = lax.rsqrt(jnp.sum(total, axis=1, keepdims=True) / features + 1e-05)
    scaled = (summed[...] * factor * gain[...]).astype(mixed.dtype)
    rows = mixed.shape[1]
    for s in range(mixed.shape[0]):
        mixed[s] = scaled[s * rows : (s + 1) * rows]
    leave[pieces].start()
    for copy in leave:
        copy.wait()


def finish(squares, summed, gain, moved, steps, features):
    rows, columns = summed.shape
    pieces = 8
    gain = gain.reshape(1, columns)
    mixed_shape = (steps, rows // steps, columns)
    shape = jax.ShapeDtypeStruct((1,) + moved.shape[1:], moved.dtype)
    return pl.pallas_call(
        functools.partial(finish_kernel, features),
        out_shape=(jax.ShapeDtypeStruct(mixed_shape, jnp.bfloat16), shape, shape),
        in_specs=[ANY, ANY, ANY, ANY],
        out_specs=(ANY, ANY, ANY),
        scratch_shapes=[
            pltpu.VMEM(squares.shape, squares.dtype),
            pltpu.VMEM(summed.shape, summed.dtype),
            pltpu.VMEM(gain.shape, gain.dtype),
            pltpu.VMEM(moved.shape, moved.dtype),
            pltpu.VMEM(mixed_shape, jnp.bfloat16),
            pltpu.SemaphoreType.DMA((3,)),
            pltpu.SemaphoreType.DMA((pieces,)),
            pltpu.SemaphoreType.DMA((pieces + 1,)),
        ],
        cost_estimate=pl.CostEstimate(flops=50_000, bytes_accessed=1 << 22, transcendentals=16),
    )(squares, summed, gain, moved)


def layer(residual, *attended):
    partial_sums = attend_project(*attended, lax.axis_size("tp"))
    parts = lax.all_to_all(partial_sums, "tp", 0, 0, tiled=True)
    summed, squares = add_parts(parts, residual)
    return (lax.all_to_all(squares, "tp", 0, 0, tiled=True), summed)


def shards(
    hidden_in,
    queries,
    new_keys,
    new_values,
    key_pool,
    value_pool,
    out_weight,
    gain,
    lengths,
    block_table,
    mig_ids,
    partner,
):
    count = lax.axis_size("replica")
    offset = jnp.bitwise_xor(partner[0], lax.axis_index("replica"))
    page_table = block_table.T
    moving, residual = gather_pages(
        page_table,
        mig_ids,
        key_pool,
        value_pool,
        hidden_in.reshape(-1, hidden_in.shape[2]),
        gain.shape[0],
    )

    def branch(distance):
        route = [(i, i ^ distance) for i in range(count)]

        def body(moving, *rest):
            moved = lax.ppermute(moving, "replica", route)
            return (*layer(*rest), moved)

        return body

    squares, summed, moved = lax.switch(
        offset - 1,
        [branch(distance) for distance in range(1, count)],
        moving, residual,
        page_table, lengths, queries, new_keys, new_values, key_pool, value_pool, out_weight,
    )
    return finish(squares, summed, gain, moved, hidden_in.shape[0], hidden_in.shape[2])


def solution(mesh):
    placed = (
        P(None, "replica", None),
        P(None, "replica", "tp"),
        P(None, "replica", "tp"),
        P(None, "replica", "tp"),
        P("tp", "replica", None, None),
        P("tp", "replica", None, None),
        P("tp", None),
        P("tp"),
        P("replica", None),
        P("replica", None),
        P("replica", None),
        P("replica"),
    )
    return jax.shard_map(
        shards,
        mesh=mesh,
        in_specs=placed,
        out_specs=(
            P(None, "replica", "tp"),
            P("tp", "replica", None, None),
            P("tp", "replica", None, None),
        ),
        check_vma=False,
    )
```

```python
import functools

import jax
import jax.numpy as jnp
from jax import lax
from jax.experimental import pallas as pl
from jax.experimental.pallas import tpu as pltpu
from jax.sharding import PartitionSpec as P

CUT = 512
VMEM = pl.BlockSpec(memory_space=pltpu.VMEM)
SMEM = pl.BlockSpec(memory_space=pltpu.SMEM)
ANY = pl.BlockSpec(memory_space=pl.ANY)
HBM = pl.BlockSpec(memory_space=pltpu.HBM)


def gather_kernel(
    table_in, ids_in, keys, values, hidden, out, residual, table, ids, scalar_sems, sems, row_sem
):
    count, pages = (ids.shape[1], table.shape[0])
    scalars = [
        pltpu.make_async_copy(table_in, table, scalar_sems.at[0]),
        pltpu.make_async_copy(ids_in, ids, scalar_sems.at[1]),
    ]
    columns = residual.shape[1]
    own = pl.ds(pl.multiple_of(lax.axis_index("tp") * columns, columns), columns)
    rows = pltpu.make_async_copy(hidden.at[:, own], residual, row_sem)
    for copy in scalars:
        copy.start()
    rows.start()
    for copy in scalars:
        copy.wait()
    for m in range(count):
        row = ids[0, m]
        for i in range(pages):
            source = pl.ds(table[i, row], 1)
            target = pl.ds(m * pages + i, 1)
            for k, pool in enumerate((keys, values)):
                pltpu.make_async_copy(
                    pool.at[:, source], out.at[pl.ds(k, 1), target], sems.at[k]
                ).start()
    for k, pool in enumerate((keys, values)):
        pltpu.make_async_copy(
            pool.at[:, pl.ds(0, count * pages)], out.at[pl.ds(k, 1)], sems.at[k]
        ).wait()
    rows.wait()


def gather_pages(block_table, mig_ids, key_pool, value_pool, hidden, columns):
    moved = mig_ids.shape[1] * block_table.shape[0]
    shape = jax.ShapeDtypeStruct((2, moved) + key_pool.shape[2:], key_pool.dtype)
    return pl.pallas_call(
        gather_kernel,
        out_shape=(shape, jax.ShapeDtypeStruct((hidden.shape[0], columns), hidden.dtype)),
        in_specs=[HBM, HBM, ANY, ANY, ANY],
        out_specs=(ANY, ANY),
        scratch_shapes=[
            pltpu.SMEM(block_table.shape, block_table.dtype),
            pltpu.SMEM(mig_ids.shape, mig_ids.dtype),
            pltpu.SemaphoreType.DMA((2,)),
            pltpu.SemaphoreType.DMA((2,)),
            pltpu.SemaphoreType.DMA,
        ],
        cost_estimate=pl.CostEstimate(flops=0, bytes_accessed=1 << 22, transcendentals=0),
    )(block_table, mig_ids, key_pool, value_pool, hidden)


def attend_kernel(
    table, lengths, queries, new_keys, new_values, keys, values, weight,
    out, key_buf, value_buf, weight_buf, query_rows, attn_rows, fresh_k, fresh_v, sems,
):
    steps, rows, width = queries.shape
    page, head = key_buf.shape[1:]
    per_group = width // head
    pages = table.shape[0]
    parts, columns = (weight_buf.shape[0], weight_buf.shape[2])

    def weight_copy(t):
        start = pl.multiple_of(t * columns, columns)
        return pltpu.make_async_copy(
            weight.at[:, pl.ds(start, columns)], weight_buf.at[t], sems.at[2 + t]
        )

    key_copy = pltpu.make_async_copy(keys.at[0], key_buf, sems.at[0])
    value_copy = pltpu.make_async_copy(values.at[0], value_buf, sems.at[1])
    key_copy.start()
    value_copy.start()
    def start_weight(t, carry):
        weight_copy(t).start()
        return carry

    lax.fori_loop(0, parts, start_weight, 0)

    for s in range(steps):
        both = queries[s].astype(jnp.float32)
        for j in range(per_group):
            query_rows[:, s * per_group + j, :] = both[:, j * head : (j + 1) * head]
        fresh_k[s] = new_keys[s].astype(jnp.float32)
        fresh_v[s] = new_values[s].astype(jnp.float32)
    scale = 1.0 / jnp.sqrt(jnp.float32(head))
    count = steps * per_group
    step_of = lax.broadcasted_iota(jnp.int32, (count, 1), 0) // per_group
    position = lax.broadcasted_iota(jnp.int32, (count, pages * page), 1)

    key_copy.wait()
    value_copy.wait()

    def attend_row(b, carry):
        query = query_rows[b]
        cached_k = jnp.concatenate([key_buf[table[i, b]] for i in range(pages)], axis=0)
        scores = lax.dot_general(
            query.astype(jnp.bfloat16),
            cached_k,
            (((1,), (1,)), ((), ())),
            preferred_element_type=jnp.float32,
        )
        scores = jnp.where(position < lengths[0, b], scores * scale, -jnp.inf)
        largest = jnp.max(scores, axis=1, keepdims=True)
        fresh = []
        for s in range(steps):
            one = jnp.sum(query * fresh_k[s, pl.ds(b, 1)], axis=1, keepdims=True) * scale
            one = jnp.where(step_of >= s, one, -jnp.inf)
            largest = jnp.maximum(largest, one)
            fresh.append(one)
        raised = jnp.exp(scores - largest)
        fresh = [jnp.exp(one - largest) for one in fresh]
        total = jnp.sum(raised, axis=1, keepdims=True)
        for one in fresh:
            total = total + one
        cached_v = jnp.concatenate([value_buf[table[i, b]] for i in range(pages)], axis=0)
        result = jnp.dot(
            (raised / total).astype(jnp.bfloat16), cached_v, preferred_element_type=jnp.float32
        )
        for s in range(steps):
            weight = (fresh[s] / total).astype(jnp.bfloat16).astype(jnp.float32)
            result = result + weight * fresh_v[s, pl.ds(b, 1)]
        attn_rows[b] = result
        return carry

    lax.fori_loop(0, rows, attend_row, 0, unroll=1)

    attn = jnp.concatenate(
        [
            jnp.concatenate([attn_rows[:, s * per_group + j, :] for j in range(per_group)], axis=1)
            for s in range(steps)
        ],
        axis=0,
    ).astype(jnp.bfloat16)

    def project(t, carry):
        weight_copy(t).wait()

        def piece(u, inner):
            at = pl.ds(pl.multiple_of(u * CUT, CUT), CUT)
            product = jnp.dot(attn, weight_buf[t, :, at], preferred_element_type=jnp.float32)
            out[t, :, at] = product.astype(out.dtype)
            return inner

        return lax.fori_loop(0, columns // CUT, piece, carry)

    lax.fori_loop(0, parts, project, 0)


def attend_project(
    block_table, lengths, queries, new_keys, new_values, key_pool, value_pool, out_weight, parts
):
    steps, rows, width = queries.shape
    pool, page, head = key_pool.shape[1:]
    columns = out_weight.shape[1] // parts
    heads = width // head
    return pl.pallas_call(
        attend_kernel,
        out_shape=jax.ShapeDtypeStruct((parts, steps * rows, columns), jnp.bfloat16),
        in_specs=[SMEM, SMEM, VMEM, VMEM, VMEM, ANY, ANY, ANY],
        out_specs=VMEM,
        scratch_shapes=[
            pltpu.VMEM((pool, page, head), key_pool.dtype),
            pltpu.VMEM((pool, page, head), value_pool.dtype),
            pltpu.VMEM((parts, width, columns), out_weight.dtype),
            pltpu.VMEM((rows, steps * heads, head), jnp.float32),
            pltpu.VMEM((rows, steps * heads, head), jnp.float32),
            pltpu.VMEM((steps, rows, head), jnp.float32),
            pltpu.VMEM((steps, rows, head), jnp.float32),
            pltpu.SemaphoreType.DMA((2 + parts,)),
        ],
        compiler_params=pltpu.CompilerParams(vmem_limit_bytes=24 << 20),
        cost_estimate=pl.CostEstimate(
            flops=160_000_000, bytes_accessed=11 << 20, transcendentals=32768
        ),
    )(block_table, lengths, queries, new_keys, new_values, key_pool, value_pool, out_weight)


def diagonal(rows):
    at = [lax.broadcasted_iota(jnp.int32, (rows, 128), axis) for axis in range(2)]
    return at[0] == at[1]


def sum_kernel(parts, residual, summed, squares):
    total = parts[0].astype(jnp.float32)
    for t in range(1, parts.shape[0]):
        total = total + parts[t].astype(jnp.float32)
    total = total + residual[...].astype(jnp.float32)
    summed[...] = total
    square = jnp.sum(total * total, axis=1, keepdims=True)
    square = jnp.sum(jnp.where(diagonal(total.shape[0]), square, 0.0), axis=0, keepdims=True)
    for t in range(squares.shape[0]):
        squares[t] = square


def add_parts(parts, residual):
    count, rows, columns = parts.shape
    return pl.pallas_call(
        sum_kernel,
        out_shape=(
            jax.ShapeDtypeStruct((rows, columns), jnp.float32),
            jax.ShapeDtypeStruct((count, 1, 128), jnp.float32),
        ),
        in_specs=[VMEM, VMEM],
        out_specs=(VMEM, VMEM),
        cost_estimate=pl.CostEstimate(flops=200_000, bytes_accessed=700_000, transcendentals=0),
    )(parts, residual)


def finish_kernel(
    features, squares_in, summed_in, gain_in, moved, mixed_out, keys_out, values_out,
    squares, summed, gain, buf, mixed, in_sems, page_sems, out_sems,
):
    pieces = page_sems.shape[0]
    per_array = pieces // 2
    size = buf.shape[1] // per_array

    def at(k):
        return (pl.ds(k // per_array, 1), pl.ds(k % per_array * size, size))

    arrive = [
        pltpu.make_async_copy(moved.at[at(k)], buf.at[at(k)], page_sems.at[k]) for k in range(pieces)
    ]
    small = [
        pltpu.make_async_copy(source, target, in_sems.at[k])
        for k, (source, target) in enumerate(
            ((squares_in, squares), (summed_in, summed), (gain_in, gain))
        )
    ]
    leave = [
        pltpu.make_async_copy(
            buf.at[at(k)],
            (keys_out, values_out)[k // per_array].at[:, pl.ds(k % per_array * size, size)],
            out_sems.at[k],
        )
        for k in range(pieces)
    ]
    leave.append(pltpu.make_async_copy(mixed, mixed_out, out_sems.at[pieces]))
    for copy in arrive + small:
        copy.start()
    for k in range(pieces):
        arrive[k].wait()
        leave[k].start()
    for copy in small:
        copy.wait()
    total = squares[0]
    for t in range(1, squares.shape[0]):
        total = total + squares[t]
    total = jnp.where(diagonal(summed.shape[0]), total, 0.0)
    factor = lax.rsqrt(jnp.sum(total, axis=1, keepdims=True) / features + 1e-05)
    scaled = (summed[...] * factor * gain[...]).astype(mixed.dtype)
    mixed[...] = scaled
    leave[pieces].start()
    for copy in leave:
        copy.wait()


def finish(squares, summed, gain, moved, steps, features):
    rows, columns = summed.shape
    pieces = 8
    gain = gain.reshape(1, columns)
    shape = jax.ShapeDtypeStruct((1,) + moved.shape[1:], moved.dtype)
    mixed, moved_keys, moved_values = pl.pallas_call(
        functools.partial(finish_kernel, features),
        out_shape=(jax.ShapeDtypeStruct(summed.shape, jnp.bfloat16), shape, shape),
        in_specs=[ANY, ANY, ANY, ANY],
        out_specs=(ANY, ANY, ANY),
        scratch_shapes=[
            pltpu.VMEM(squares.shape, squares.dtype),
            pltpu.VMEM(summed.shape, summed.dtype),
            pltpu.VMEM(gain.shape, gain.dtype),
            pltpu.VMEM(moved.shape, moved.dtype),
            pltpu.VMEM(summed.shape, jnp.bfloat16),
            pltpu.SemaphoreType.DMA((3,)),
            pltpu.SemaphoreType.DMA((pieces,)),
            pltpu.SemaphoreType.DMA((pieces + 1,)),
        ],
        cost_estimate=pl.CostEstimate(flops=50_000, bytes_accessed=1 << 22, transcendentals=16),
    )(squares, summed, gain, moved)
    return (mixed.reshape(steps, rows // steps, columns), moved_keys, moved_values)


def layer(residual, *attended):
    partial_sums = attend_project(*attended, lax.axis_size("tp"))
    parts = lax.all_to_all(partial_sums, "tp", 0, 0, tiled=True)
    summed, squares = add_parts(parts, residual)
    return (lax.all_to_all(squares, "tp", 0, 0, tiled=True), summed)


def shards(
    hidden_in,
    queries,
    new_keys,
    new_values,
    key_pool,
    value_pool,
    out_weight,
    gain,
    lengths,
    block_table,
    mig_ids,
    partner,
):
    count = lax.axis_size("replica")
    offset = jnp.bitwise_xor(partner[0], lax.axis_index("replica"))
    page_table = block_table.T
    moving, residual = gather_pages(
        page_table,
        mig_ids,
        key_pool,
        value_pool,
        hidden_in.reshape(-1, hidden_in.shape[2]),
        gain.shape[0],
    )

    def branch(distance):
        route = [(i, i ^ distance) for i in range(count)]

        def body(moving, *rest):
            moved = lax.ppermute(moving, "replica", route)
            return (*layer(*rest), moved)

        return body

    squares, summed, moved = lax.switch(
        offset - 1,
        [branch(distance) for distance in range(1, count)],
        moving, residual,
        page_table, lengths, queries, new_keys, new_values, key_pool, value_pool, out_weight,
    )
    return finish(squares, summed, gain, moved, hidden_in.shape[0], hidden_in.shape[2])


def solution(mesh):
    placed = (
        P(None, "replica", None),
        P(None, "replica", "tp"),
        P(None, "replica", "tp"),
        P(None, "replica", "tp"),
        P("tp", "replica", None, None),
        P("tp", "replica", None, None),
        P("tp", None),
        P("tp"),
        P("replica", None),
        P("replica", None),
        P("replica", None),
        P("replica"),
    )
    return jax.shard_map(
        shards,
        mesh=mesh,
        in_specs=placed,
        out_specs=(
            P(None, "replica", "tp"),
            P("tp", "replica", None, None),
            P("tp", "replica", None, None),
        ),
        check_vma=False,
    )
```

```python
import functools

import jax
import jax.numpy as jnp
from jax import lax
from jax.experimental import pallas as pl
from jax.experimental.pallas import tpu as pltpu
from jax.sharding import PartitionSpec as P

SHORT = (1, 4, 5)
VMEM = pl.BlockSpec(memory_space=pltpu.VMEM)
SMEM = pl.BlockSpec(memory_space=pltpu.SMEM)
ANY = pl.BlockSpec(memory_space=pl.ANY)
HBM = pl.BlockSpec(memory_space=pltpu.HBM)


def gather_kernel(
    table_in, ids_in, keys, values, hidden, out, residual, table, ids, scalar_sems, sems, row_sem
):
    count, pages = (ids.shape[1], table.shape[0])
    scalars = [
        pltpu.make_async_copy(table_in, table, scalar_sems.at[0]),
        pltpu.make_async_copy(ids_in, ids, scalar_sems.at[1]),
    ]
    columns = residual.shape[1]
    own = pl.ds(pl.multiple_of(lax.axis_index("tp") * columns, columns), columns)
    rows = pltpu.make_async_copy(hidden.at[:, own], residual, row_sem)
    for copy in scalars:
        copy.start()
    rows.start()
    for copy in scalars:
        copy.wait()
    for m in range(count):
        row = ids[0, m]
        for i in range(pages):
            source = pl.ds(table[i, row], 1)
            target = pl.ds(m * pages + i, 1)
            for k, pool in enumerate((keys, values)):
                pltpu.make_async_copy(
                    pool.at[:, source], out.at[pl.ds(k, 1), target], sems.at[k]
                ).start()
    for k, pool in enumerate((keys, values)):
        pltpu.make_async_copy(
            pool.at[:, pl.ds(0, count * pages)], out.at[pl.ds(k, 1)], sems.at[k]
        ).wait()
    rows.wait()


def gather_pages(block_table, mig_ids, key_pool, value_pool, hidden, columns):
    moved = mig_ids.shape[1] * block_table.shape[0]
    shape = jax.ShapeDtypeStruct((2, moved) + key_pool.shape[2:], key_pool.dtype)
    return pl.pallas_call(
        gather_kernel,
        out_shape=(shape, jax.ShapeDtypeStruct((hidden.shape[0], columns), hidden.dtype)),
        in_specs=[HBM, HBM, ANY, ANY, ANY],
        out_specs=(ANY, ANY),
        scratch_shapes=[
            pltpu.SMEM(block_table.shape, block_table.dtype),
            pltpu.SMEM(mig_ids.shape, mig_ids.dtype),
            pltpu.SemaphoreType.DMA((2,)),
            pltpu.SemaphoreType.DMA((2,)),
            pltpu.SemaphoreType.DMA,
        ],
        cost_estimate=pl.CostEstimate(flops=0, bytes_accessed=1 << 22, transcendentals=0),
    )(block_table, mig_ids, key_pool, value_pool, hidden)


def attend_kernel(
    cut, unroll, table, lengths, queries, new_keys, new_values, keys, values, weight,
    out, key_buf, value_buf, weight_buf, query_rows, attn_rows, fresh_k, fresh_v, sems,
):
    steps, rows, width = queries.shape
    page, head = key_buf.shape[1:]
    per_group = width // head
    pages = table.shape[0]
    parts, columns = (weight_buf.shape[0], weight_buf.shape[2])

    def weight_copy(t):
        start = pl.multiple_of(t * columns, columns)
        return pltpu.make_async_copy(
            weight.at[:, pl.ds(start, columns)], weight_buf.at[t], sems.at[2 + t]
        )

    key_copy = pltpu.make_async_copy(keys.at[0], key_buf, sems.at[0])
    value_copy = pltpu.make_async_copy(values.at[0], value_buf, sems.at[1])
    key_copy.start()
    value_copy.start()
    def start_weight(t, carry):
        weight_copy(t).start()
        return carry

    lax.fori_loop(0, parts, start_weight, 0)

    for s in range(steps):
        both = queries[s].astype(jnp.float32)
        for j in range(per_group):
            query_rows[:, s * per_group + j, :] = both[:, j * head : (j + 1) * head]
        fresh_k[s] = new_keys[s].astype(jnp.float32)
        fresh_v[s] = new_values[s].astype(jnp.float32)
    scale = 1.0 / jnp.sqrt(jnp.float32(head))
    count = steps * per_group
    step_of = lax.broadcasted_iota(jnp.int32, (count, 1), 0) // per_group
    position = lax.broadcasted_iota(jnp.int32, (count, pages * page), 1)

    key_copy.wait()
    value_copy.wait()

    def attend_row(b, carry):
        query = query_rows[b]
        cached_k = jnp.concatenate([key_buf[table[i, b]] for i in range(pages)], axis=0)
        scores = lax.dot_general(
            query.astype(jnp.bfloat16),
            cached_k,
            (((1,), (1,)), ((), ())),
            preferred_element_type=jnp.float32,
        )
        scores = jnp.where(position < lengths[0, b], scores * scale, -jnp.inf)
        largest = jnp.max(scores, axis=1, keepdims=True)
        fresh = []
        for s in range(steps):
            one = jnp.sum(query * fresh_k[s, pl.ds(b, 1)], axis=1, keepdims=True) * scale
            one = jnp.where(step_of >= s, one, -jnp.inf)
            largest = jnp.maximum(largest, one)
            fresh.append(one)
        raised = jnp.exp(scores - largest)
        fresh = [jnp.exp(one - largest) for one in fresh]
        total = jnp.sum(raised, axis=1, keepdims=True)
        for one in fresh:
            total = total + one
        cached_v = jnp.concatenate([value_buf[table[i, b]] for i in range(pages)], axis=0)
        result = jnp.dot(
            (raised / total).astype(jnp.bfloat16), cached_v, preferred_element_type=jnp.float32
        )
        for s in range(steps):
            weight = (fresh[s] / total).astype(jnp.bfloat16).astype(jnp.float32)
            result = result + weight * fresh_v[s, pl.ds(b, 1)]
        attn_rows[b] = result
        return carry

    lax.fori_loop(0, rows, attend_row, 0, unroll=unroll)

    attn = jnp.concatenate(
        [
            jnp.concatenate([attn_rows[:, s * per_group + j, :] for j in range(per_group)], axis=1)
            for s in range(steps)
        ],
        axis=0,
    ).astype(jnp.bfloat16)

    def project(t, carry):
        weight_copy(t).wait()

        def piece(u, inner):
            at = pl.ds(pl.multiple_of(u * cut, cut), cut)
            product = jnp.dot(attn, weight_buf[t, :, at], preferred_element_type=jnp.float32)
            out[t, :, at] = product.astype(out.dtype)
            return inner

        return lax.fori_loop(0, columns // cut, piece, carry)

    lax.fori_loop(0, parts, project, 0)


def attend_project(
    cut, unroll, parts, block_table, lengths, queries, new_keys, new_values, key_pool, value_pool, out_weight
):
    steps, rows, width = queries.shape
    pool, page, head = key_pool.shape[1:]
    columns = out_weight.shape[1] // parts
    heads = width // head
    return pl.pallas_call(
        functools.partial(attend_kernel, cut, unroll),
        out_shape=jax.ShapeDtypeStruct((parts, steps * rows, columns), jnp.bfloat16),
        in_specs=[SMEM, SMEM, VMEM, VMEM, VMEM, ANY, ANY, ANY],
        out_specs=VMEM,
        scratch_shapes=[
            pltpu.VMEM((pool, page, head), key_pool.dtype),
            pltpu.VMEM((pool, page, head), value_pool.dtype),
            pltpu.VMEM((parts, width, columns), out_weight.dtype),
            pltpu.VMEM((rows, steps * heads, head), jnp.float32),
            pltpu.VMEM((rows, steps * heads, head), jnp.float32),
            pltpu.VMEM((steps, rows, head), jnp.float32),
            pltpu.VMEM((steps, rows, head), jnp.float32),
            pltpu.SemaphoreType.DMA((2 + parts,)),
        ],
        compiler_params=pltpu.CompilerParams(vmem_limit_bytes=24 << 20),
        cost_estimate=pl.CostEstimate(
            flops=160_000_000, bytes_accessed=11 << 20, transcendentals=32768
        ),
    )(block_table, lengths, queries, new_keys, new_values, key_pool, value_pool, out_weight)


def diagonal(rows):
    at = [lax.broadcasted_iota(jnp.int32, (rows, 128), axis) for axis in range(2)]
    return at[0] == at[1]


def sum_kernel(parts, residual, summed, squares):
    def add(t, total):
        return total + parts[t].astype(jnp.float32)

    total = lax.fori_loop(0, parts.shape[0], add, residual[...].astype(jnp.float32))
    summed[...] = total
    square = jnp.sum(total * total, axis=1, keepdims=True)
    square = jnp.sum(jnp.where(diagonal(total.shape[0]), square, 0.0), axis=0, keepdims=True)
    for t in range(squares.shape[0]):
        squares[t] = square


def add_parts(parts, residual):
    count, rows, columns = parts.shape
    return pl.pallas_call(
        sum_kernel,
        out_shape=(
            jax.ShapeDtypeStruct((rows, columns), jnp.float32),
            jax.ShapeDtypeStruct((count, 1, 128), jnp.float32),
        ),
        in_specs=[VMEM, VMEM],
        out_specs=(VMEM, VMEM),
        cost_estimate=pl.CostEstimate(flops=200_000, bytes_accessed=700_000, transcendentals=0),
    )(parts, residual)


def finish_kernel(
    features, squares_in, summed_in, gain_in, moved, mixed_out, keys_out, values_out,
    squares, summed, gain, buf, mixed, in_sems, page_sems, out_sems,
):
    pieces = page_sems.shape[0]
    per_array = pieces // 2
    size = buf.shape[1] // per_array

    def at(k):
        return (pl.ds(k // per_array, 1), pl.ds(k % per_array * size, size))

    arrive = [
        pltpu.make_async_copy(moved.at[at(k)], buf.at[at(k)], page_sems.at[k]) for k in range(pieces)
    ]
    small = [
        pltpu.make_async_copy(source, target, in_sems.at[k])
        for k, (source, target) in enumerate(
            ((squares_in, squares), (summed_in, summed), (gain_in, gain))
        )
    ]
    leave = [
        pltpu.make_async_copy(
            buf.at[at(k)],
            (keys_out, values_out)[k // per_array].at[:, pl.ds(k % per_array * size, size)],
            out_sems.at[k],
        )
        for k in range(pieces)
    ]
    leave.append(pltpu.make_async_copy(mixed, mixed_out, out_sems.at[pieces]))
    for copy in arrive + small:
        copy.start()
    for k in range(pieces):
        arrive[k].wait()
        leave[k].start()
    for copy in small:
        copy.wait()
    total = squares[0]
    for t in range(1, squares.shape[0]):
        total = total + squares[t]
    total = jnp.where(diagonal(summed.shape[0]), total, 0.0)
    factor = lax.rsqrt(jnp.sum(total, axis=1, keepdims=True) / features + 1e-05)
    scaled = (summed[...] * factor * gain[...]).astype(mixed.dtype)
    mixed[...] = scaled
    leave[pieces].start()
    for copy in leave:
        copy.wait()


def finish(squares, summed, gain, moved, steps, features):
    rows, columns = summed.shape
    pieces = 8
    gain = gain.reshape(1, columns)
    shape = jax.ShapeDtypeStruct((1,) + moved.shape[1:], moved.dtype)
    mixed, moved_keys, moved_values = pl.pallas_call(
        functools.partial(finish_kernel, features),
        out_shape=(jax.ShapeDtypeStruct(summed.shape, jnp.bfloat16), shape, shape),
        in_specs=[ANY, ANY, ANY, ANY],
        out_specs=(ANY, ANY, ANY),
        scratch_shapes=[
            pltpu.VMEM(squares.shape, squares.dtype),
            pltpu.VMEM(summed.shape, summed.dtype),
            pltpu.VMEM(gain.shape, gain.dtype),
            pltpu.VMEM(moved.shape, moved.dtype),
            pltpu.VMEM(summed.shape, jnp.bfloat16),
            pltpu.SemaphoreType.DMA((3,)),
            pltpu.SemaphoreType.DMA((pieces,)),
            pltpu.SemaphoreType.DMA((pieces + 1,)),
        ],
        cost_estimate=pl.CostEstimate(flops=50_000, bytes_accessed=1 << 22, transcendentals=16),
    )(squares, summed, gain, moved)
    return (mixed.reshape(steps, rows // steps, columns), moved_keys, moved_values)


def layer(short, residual, *attended):
    cut, unroll = (1024, 4) if short else (512, 1)
    partial_sums = attend_project(cut, unroll, lax.axis_size("tp"), *attended)
    parts = lax.all_to_all(partial_sums, "tp", 0, 0, tiled=True)
    summed, squares = add_parts(parts, residual)
    return (lax.all_to_all(squares, "tp", 0, 0, tiled=True), summed)


def shards(
    hidden_in,
    queries,
    new_keys,
    new_values,
    key_pool,
    value_pool,
    out_weight,
    gain,
    lengths,
    block_table,
    mig_ids,
    partner,
):
    count = lax.axis_size("replica")
    offset = jnp.bitwise_xor(partner[0], lax.axis_index("replica"))
    page_table = block_table.T
    moving, residual = gather_pages(
        page_table,
        mig_ids,
        key_pool,
        value_pool,
        hidden_in.reshape(-1, hidden_in.shape[2]),
        gain.shape[0],
    )

    def branch(distance):
        route = [(i, i ^ distance) for i in range(count)]
        short = distance in SHORT

        def body(moving, *rest):
            moved = lax.ppermute(moving, "replica", route)
            return (*layer(short, *rest), moved)

        return body

    squares, summed, moved = lax.switch(
        offset - 1,
        [branch(distance) for distance in range(1, count)],
        moving, residual,
        page_table, lengths, queries, new_keys, new_values, key_pool, value_pool, out_weight,
    )
    return finish(squares, summed, gain, moved, hidden_in.shape[0], hidden_in.shape[2])


def solution(mesh):
    placed = (
        P(None, "replica", None),
        P(None, "replica", "tp"),
        P(None, "replica", "tp"),
        P(None, "replica", "tp"),
        P("tp", "replica", None, None),
        P("tp", "replica", None, None),
        P("tp", None),
        P("tp"),
        P("replica", None),
        P("replica", None),
        P("replica", None),
        P("replica"),
    )
    return jax.shard_map(
        shards,
        mesh=mesh,
        in_specs=placed,
        out_specs=(
            P(None, "replica", "tp"),
            P("tp", "replica", None, None),
            P("tp", "replica", None, None),
        ),
        check_vma=False,
    )
```

```python
import functools

import jax
import jax.numpy as jnp
from jax import lax
from jax.experimental import pallas as pl
from jax.experimental.pallas import tpu as pltpu
from jax.sharding import PartitionSpec as P

SHORT = (1, 4, 5)
VMEM = pl.BlockSpec(memory_space=pltpu.VMEM)
SMEM = pl.BlockSpec(memory_space=pltpu.SMEM)
ANY = pl.BlockSpec(memory_space=pl.ANY)
HBM = pl.BlockSpec(memory_space=pltpu.HBM)


def gather_kernel(
    table_in, ids_in, keys, values, hidden, out, residual, table, ids, scalar_sems, sems, row_sem
):
    count, pages = (ids.shape[1], table.shape[0])
    scalars = [
        pltpu.make_async_copy(table_in, table, scalar_sems.at[0]),
        pltpu.make_async_copy(ids_in, ids, scalar_sems.at[1]),
    ]
    columns = residual.shape[1]
    own = pl.ds(pl.multiple_of(lax.axis_index("tp") * columns, columns), columns)
    rows = pltpu.make_async_copy(hidden.at[:, own], residual, row_sem)
    for copy in scalars:
        copy.start()
    rows.start()
    for copy in scalars:
        copy.wait()
    for m in range(count):
        row = ids[0, m]
        for i in range(pages):
            source = pl.ds(table[i, row], 1)
            target = pl.ds(m * pages + i, 1)
            for k, pool in enumerate((keys, values)):
                pltpu.make_async_copy(
                    pool.at[:, source], out.at[pl.ds(k, 1), target], sems.at[k]
                ).start()
    for k, pool in enumerate((keys, values)):
        pltpu.make_async_copy(
            pool.at[:, pl.ds(0, count * pages)], out.at[pl.ds(k, 1)], sems.at[k]
        ).wait()
    rows.wait()


def gather_pages(block_table, mig_ids, key_pool, value_pool, hidden, columns):
    moved = mig_ids.shape[1] * block_table.shape[0]
    shape = jax.ShapeDtypeStruct((2, moved) + key_pool.shape[2:], key_pool.dtype)
    return pl.pallas_call(
        gather_kernel,
        out_shape=(shape, jax.ShapeDtypeStruct((hidden.shape[0], columns), hidden.dtype)),
        in_specs=[HBM, HBM, ANY, ANY, ANY],
        out_specs=(ANY, ANY),
        scratch_shapes=[
            pltpu.SMEM(block_table.shape, block_table.dtype),
            pltpu.SMEM(mig_ids.shape, mig_ids.dtype),
            pltpu.SemaphoreType.DMA((2,)),
            pltpu.SemaphoreType.DMA((2,)),
            pltpu.SemaphoreType.DMA,
        ],
        cost_estimate=pl.CostEstimate(flops=0, bytes_accessed=1 << 22, transcendentals=0),
    )(block_table, mig_ids, key_pool, value_pool, hidden)


def attend_kernel(
    cut, unroll, table, lengths, queries, new_keys, new_values, keys, values, weight,
    out, key_buf, value_buf, weight_buf, query_rows, attn_rows, fresh_k, fresh_v, sems,
):
    steps, rows, width = queries.shape
    page, head = key_buf.shape[1:]
    per_group = width // head
    pages = table.shape[0]
    parts, columns = (weight_buf.shape[0], weight_buf.shape[2])

    def weight_copy(t):
        start = pl.multiple_of(t * columns, columns)
        return pltpu.make_async_copy(
            weight.at[:, pl.ds(start, columns)], weight_buf.at[t], sems.at[2 + t]
        )

    key_copy = pltpu.make_async_copy(keys.at[0], key_buf, sems.at[0])
    value_copy = pltpu.make_async_copy(values.at[0], value_buf, sems.at[1])
    key_copy.start()
    value_copy.start()
    def start_weight(t, carry):
        weight_copy(t).start()
        return carry

    lax.fori_loop(0, parts, start_weight, 0)

    for s in range(steps):
        both = queries[s].astype(jnp.float32)
        for j in range(per_group):
            query_rows[:, s * per_group + j, :] = both[:, j * head : (j + 1) * head]
        fresh_k[s] = new_keys[s].astype(jnp.float32)
        fresh_v[s] = new_values[s].astype(jnp.float32)
    scale = 1.0 / jnp.sqrt(jnp.float32(head))
    count = steps * per_group
    step_of = lax.broadcasted_iota(jnp.int32, (count, 1), 0) // per_group
    position = lax.broadcasted_iota(jnp.int32, (count, pages * page), 1)

    key_copy.wait()
    value_copy.wait()

    def attend_row(b, carry):
        query = query_rows[b]
        cached_k = jnp.concatenate([key_buf[table[i, b]] for i in range(pages)], axis=0)
        scores = lax.dot_general(
            query.astype(jnp.bfloat16),
            cached_k,
            (((1,), (1,)), ((), ())),
            preferred_element_type=jnp.float32,
        )
        scores = jnp.where(position < lengths[0, b], scores * scale, -jnp.inf)
        largest = jnp.max(scores, axis=1, keepdims=True)
        fresh = []
        for s in range(steps):
            one = jnp.sum(query * fresh_k[s, pl.ds(b, 1)], axis=1, keepdims=True) * scale
            one = jnp.where(step_of >= s, one, -jnp.inf)
            largest = jnp.maximum(largest, one)
            fresh.append(one)
        raised = jnp.exp(scores - largest)
        fresh = [jnp.exp(one - largest) for one in fresh]
        total = jnp.sum(raised, axis=1, keepdims=True)
        for one in fresh:
            total = total + one
        cached_v = jnp.concatenate([value_buf[table[i, b]] for i in range(pages)], axis=0)
        result = jnp.dot(
            (raised / total).astype(jnp.bfloat16), cached_v, preferred_element_type=jnp.float32
        )
        for s in range(steps):
            weight = (fresh[s] / total).astype(jnp.bfloat16).astype(jnp.float32)
            result = result + weight * fresh_v[s, pl.ds(b, 1)]
        attn_rows[b] = result
        return carry

    lax.fori_loop(0, rows, attend_row, 0, unroll=unroll)

    attn = jnp.concatenate(
        [
            jnp.concatenate([attn_rows[:, s * per_group + j, :] for j in range(per_group)], axis=1)
            for s in range(steps)
        ],
        axis=0,
    ).astype(jnp.bfloat16)

    def project(t, carry):
        weight_copy(t).wait()

        def piece(u, inner):
            at = pl.ds(pl.multiple_of(u * cut, cut), cut)
            product = jnp.dot(attn, weight_buf[t, :, at], preferred_element_type=jnp.float32)
            out[t, :, at] = product.astype(out.dtype)
            return inner

        return lax.fori_loop(0, columns // cut, piece, carry)

    lax.fori_loop(0, parts, project, 0)


def attend_project(
    cut, unroll, parts, block_table, lengths, queries, new_keys, new_values, key_pool, value_pool, out_weight
):
    steps, rows, width = queries.shape
    pool, page, head = key_pool.shape[1:]
    columns = out_weight.shape[1] // parts
    heads = width // head
    return pl.pallas_call(
        functools.partial(attend_kernel, cut, unroll),
        out_shape=jax.ShapeDtypeStruct((parts, steps * rows, columns), jnp.bfloat16),
        in_specs=[SMEM, SMEM, VMEM, VMEM, VMEM, ANY, ANY, ANY],
        out_specs=VMEM,
        scratch_shapes=[
            pltpu.VMEM((pool, page, head), key_pool.dtype),
            pltpu.VMEM((pool, page, head), value_pool.dtype),
            pltpu.VMEM((parts, width, columns), out_weight.dtype),
            pltpu.VMEM((rows, steps * heads, head), jnp.float32),
            pltpu.VMEM((rows, steps * heads, head), jnp.float32),
            pltpu.VMEM((steps, rows, head), jnp.float32),
            pltpu.VMEM((steps, rows, head), jnp.float32),
            pltpu.SemaphoreType.DMA((2 + parts,)),
        ],
        compiler_params=pltpu.CompilerParams(vmem_limit_bytes=24 << 20),
        cost_estimate=pl.CostEstimate(
            flops=160_000_000, bytes_accessed=11 << 20, transcendentals=32768
        ),
    )(block_table, lengths, queries, new_keys, new_values, key_pool, value_pool, out_weight)


def diagonal(rows):
    at = [lax.broadcasted_iota(jnp.int32, (rows, 128), axis) for axis in range(2)]
    return at[0] == at[1]


def sum_kernel(parts, residual, summed, squares):
    def add(t, total):
        return total + parts[t].astype(jnp.float32)

    total = lax.fori_loop(0, parts.shape[0], add, residual[...].astype(jnp.float32))
    summed[...] = total
    square = jnp.sum(total * total, axis=1, keepdims=True)
    square = jnp.sum(jnp.where(diagonal(total.shape[0]), square, 0.0), axis=0, keepdims=True)
    for t in range(squares.shape[0]):
        squares[t] = square


def add_parts(parts, residual):
    count, rows, columns = parts.shape
    return pl.pallas_call(
        sum_kernel,
        out_shape=(
            jax.ShapeDtypeStruct((rows, columns), jnp.float32),
            jax.ShapeDtypeStruct((count, 1, 128), jnp.float32),
        ),
        in_specs=[VMEM, VMEM],
        out_specs=(VMEM, VMEM),
        cost_estimate=pl.CostEstimate(flops=200_000, bytes_accessed=700_000, transcendentals=0),
    )(parts, residual)


def finish_kernel(
    features, squares_in, summed_in, gain_in, moved, mixed_out, keys_out, values_out,
    squares, summed, gain, buf, mixed, in_sems, page_sems, out_sems,
):
    pieces = page_sems.shape[0]
    per_array = pieces // 2
    size = buf.shape[1] // per_array

    def at(k):
        return (pl.ds(k // per_array, 1), pl.ds(k % per_array * size, size))

    arrive = [
        pltpu.make_async_copy(moved.at[at(k)], buf.at[at(k)], page_sems.at[k]) for k in range(pieces)
    ]
    small = [
        pltpu.make_async_copy(source, target, in_sems.at[k])
        for k, (source, target) in enumerate(
            ((squares_in, squares), (summed_in, summed), (gain_in, gain))
        )
    ]
    leave = [
        pltpu.make_async_copy(
            buf.at[at(k)],
            (keys_out, values_out)[k // per_array].at[:, pl.ds(k % per_array * size, size)],
            out_sems.at[k],
        )
        for k in range(pieces)
    ]
    leave.append(pltpu.make_async_copy(mixed, mixed_out, out_sems.at[pieces]))
    for copy in arrive + small:
        copy.start()
    for k in range(pieces):
        arrive[k].wait()
        leave[k].start()
    for copy in small:
        copy.wait()
    total = squares[0]
    for t in range(1, squares.shape[0]):
        total = total + squares[t]
    total = jnp.where(diagonal(summed.shape[0]), total, 0.0)
    factor = lax.rsqrt(jnp.sum(total, axis=1, keepdims=True) / features + 1e-05)
    scaled = (summed[...] * factor * gain[...]).astype(mixed.dtype)
    mixed[...] = scaled
    leave[pieces].start()
    for copy in leave:
        copy.wait()


def finish(squares, summed, gain, moved, steps, features):
    rows, columns = summed.shape
    pieces = 4
    gain = gain.reshape(1, columns)
    shape = jax.ShapeDtypeStruct((1,) + moved.shape[1:], moved.dtype)
    mixed, moved_keys, moved_values = pl.pallas_call(
        functools.partial(finish_kernel, features),
        out_shape=(jax.ShapeDtypeStruct(summed.shape, jnp.bfloat16), shape, shape),
        in_specs=[ANY, ANY, ANY, ANY],
        out_specs=(ANY, ANY, ANY),
        scratch_shapes=[
            pltpu.VMEM(squares.shape, squares.dtype),
            pltpu.VMEM(summed.shape, summed.dtype),
            pltpu.VMEM(gain.shape, gain.dtype),
            pltpu.VMEM(moved.shape, moved.dtype),
            pltpu.VMEM(summed.shape, jnp.bfloat16),
            pltpu.SemaphoreType.DMA((3,)),
            pltpu.SemaphoreType.DMA((pieces,)),
            pltpu.SemaphoreType.DMA((pieces + 1,)),
        ],
        cost_estimate=pl.CostEstimate(flops=50_000, bytes_accessed=1 << 22, transcendentals=16),
    )(squares, summed, gain, moved)
    return (mixed.reshape(steps, rows // steps, columns), moved_keys, moved_values)


def layer(short, residual, *attended):
    cut, unroll = (1024, 4) if short else (512, 1)
    partial_sums = attend_project(cut, unroll, lax.axis_size("tp"), *attended)
    parts = lax.all_to_all(partial_sums, "tp", 0, 0, tiled=True)
    summed, squares = add_parts(parts, residual)
    return (lax.all_to_all(squares, "tp", 0, 0, tiled=True), summed)


def shards(
    hidden_in,
    queries,
    new_keys,
    new_values,
    key_pool,
    value_pool,
    out_weight,
    gain,
    lengths,
    block_table,
    mig_ids,
    partner,
):
    count = lax.axis_size("replica")
    offset = jnp.bitwise_xor(partner[0], lax.axis_index("replica"))
    page_table = block_table.T
    moving, residual = gather_pages(
        page_table,
        mig_ids,
        key_pool,
        value_pool,
        hidden_in.reshape(-1, hidden_in.shape[2]),
        gain.shape[0],
    )

    def branch(distance):
        route = [(i, i ^ distance) for i in range(count)]
        short = distance in SHORT

        def body(moving, *rest):
            moved = lax.ppermute(moving, "replica", route)
            return (*layer(short, *rest), moved)

        return body

    squares, summed, moved = lax.switch(
        offset - 1,
        [branch(distance) for distance in range(1, count)],
        moving, residual,
        page_table, lengths, queries, new_keys, new_values, key_pool, value_pool, out_weight,
    )
    return finish(squares, summed, gain, moved, hidden_in.shape[0], hidden_in.shape[2])


def solution(mesh):
    placed = (
        P(None, "replica", None),
        P(None, "replica", "tp"),
        P(None, "replica", "tp"),
        P(None, "replica", "tp"),
        P("tp", "replica", None, None),
        P("tp", "replica", None, None),
        P("tp", None),
        P("tp"),
        P("replica", None),
        P("replica", None),
        P("replica", None),
        P("replica"),
    )
    return jax.shard_map(
        shards,
        mesh=mesh,
        in_specs=placed,
        out_specs=(
            P(None, "replica", "tp"),
            P("tp", "replica", None, None),
            P("tp", "replica", None, None),
        ),
        check_vma=False,
    )
```

```python
import functools

import jax
import jax.numpy as jnp
from jax import lax
from jax.experimental import pallas as pl
from jax.experimental.pallas import tpu as pltpu
from jax.sharding import PartitionSpec as P

SHORT = (1, 4, 5)
VMEM = pl.BlockSpec(memory_space=pltpu.VMEM)
SMEM = pl.BlockSpec(memory_space=pltpu.SMEM)
ANY = pl.BlockSpec(memory_space=pl.ANY)
HBM = pl.BlockSpec(memory_space=pltpu.HBM)


def gather_kernel(
    table_in, ids_in, keys, values, hidden, out, residual, table, ids, scalar_sems, sems, row_sem
):
    count, pages = (ids.shape[1], table.shape[0])
    scalars = [
        pltpu.make_async_copy(table_in, table, scalar_sems.at[0]),
        pltpu.make_async_copy(ids_in, ids, scalar_sems.at[1]),
    ]
    columns = residual.shape[1]
    own = pl.ds(pl.multiple_of(lax.axis_index("tp") * columns, columns), columns)
    rows = pltpu.make_async_copy(hidden.at[:, own], residual, row_sem)
    for copy in scalars:
        copy.start()
    rows.start()
    for copy in scalars:
        copy.wait()
    for m in range(count):
        row = ids[0, m]
        for i in range(pages):
            source = pl.ds(table[i, row], 1)
            target = pl.ds(m * pages + i, 1)
            for k, pool in enumerate((keys, values)):
                pltpu.make_async_copy(
                    pool.at[:, source], out.at[pl.ds(k, 1), target], sems.at[k]
                ).start()
    for k, pool in enumerate((keys, values)):
        pltpu.make_async_copy(
            pool.at[:, pl.ds(0, count * pages)], out.at[pl.ds(k, 1)], sems.at[k]
        ).wait()
    rows.wait()


def gather_pages(block_table, mig_ids, key_pool, value_pool, hidden, columns):
    moved = mig_ids.shape[1] * block_table.shape[0]
    shape = jax.ShapeDtypeStruct((2, moved) + key_pool.shape[2:], key_pool.dtype)
    return pl.pallas_call(
        gather_kernel,
        out_shape=(shape, jax.ShapeDtypeStruct((hidden.shape[0], columns), hidden.dtype)),
        in_specs=[HBM, HBM, ANY, ANY, ANY],
        out_specs=(ANY, ANY),
        scratch_shapes=[
            pltpu.SMEM(block_table.shape, block_table.dtype),
            pltpu.SMEM(mig_ids.shape, mig_ids.dtype),
            pltpu.SemaphoreType.DMA((2,)),
            pltpu.SemaphoreType.DMA((2,)),
            pltpu.SemaphoreType.DMA,
        ],
        cost_estimate=pl.CostEstimate(flops=0, bytes_accessed=1 << 22, transcendentals=0),
    )(block_table, mig_ids, key_pool, value_pool, hidden)


def attend_kernel(
    cut, unroll, table, lengths, queries, new_keys, new_values, keys, values, weight,
    out, key_buf, value_buf, weight_buf, query_rows, attn_rows, fresh_k, fresh_v, sems,
):
    steps, rows, width = queries.shape
    page, head = key_buf.shape[1:]
    per_group = width // head
    pages = table.shape[0]
    parts, columns = (weight_buf.shape[0], weight_buf.shape[2])

    def weight_copy(t):
        start = pl.multiple_of(t * columns, columns)
        return pltpu.make_async_copy(
            weight.at[:, pl.ds(start, columns)], weight_buf.at[t], sems.at[2 + t]
        )

    key_copy = pltpu.make_async_copy(keys.at[0], key_buf, sems.at[0])
    value_copy = pltpu.make_async_copy(values.at[0], value_buf, sems.at[1])
    key_copy.start()
    value_copy.start()
    def start_weight(t, carry):
        weight_copy(t).start()
        return carry

    lax.fori_loop(0, parts, start_weight, 0)

    for s in range(steps):
        both = queries[s].astype(jnp.float32)
        for j in range(per_group):
            query_rows[:, s * per_group + j, :] = both[:, j * head : (j + 1) * head]
        fresh_k[s] = new_keys[s].astype(jnp.float32)
        fresh_v[s] = new_values[s].astype(jnp.float32)
    scale = 1.0 / jnp.sqrt(jnp.float32(head))
    count = steps * per_group
    step_of = lax.broadcasted_iota(jnp.int32, (count, 1), 0) // per_group
    position = lax.broadcasted_iota(jnp.int32, (count, pages * page), 1)

    key_copy.wait()
    value_copy.wait()

    def attend_row(b, carry):
        query = query_rows[b]
        cached_k = jnp.concatenate([key_buf[table[i, b]] for i in range(pages)], axis=0)
        scores = lax.dot_general(
            query.astype(jnp.bfloat16),
            cached_k,
            (((1,), (1,)), ((), ())),
            preferred_element_type=jnp.float32,
        )
        scores = jnp.where(position < lengths[0, b], scores * scale, -jnp.inf)
        largest = jnp.max(scores, axis=1, keepdims=True)
        fresh = []
        for s in range(steps):
            one = jnp.sum(query * fresh_k[s, pl.ds(b, 1)], axis=1, keepdims=True) * scale
            one = jnp.where(step_of >= s, one, -jnp.inf)
            largest = jnp.maximum(largest, one)
            fresh.append(one)
        raised = jnp.exp(scores - largest)
        fresh = [jnp.exp(one - largest) for one in fresh]
        total = jnp.sum(raised, axis=1, keepdims=True)
        for one in fresh:
            total = total + one
        cached_v = jnp.concatenate([value_buf[table[i, b]] for i in range(pages)], axis=0)
        result = jnp.dot(
            (raised / total).astype(jnp.bfloat16), cached_v, preferred_element_type=jnp.float32
        )
        for s in range(steps):
            weight = (fresh[s] / total).astype(jnp.bfloat16).astype(jnp.float32)
            result = result + weight * fresh_v[s, pl.ds(b, 1)]
        attn_rows[b] = result
        return carry

    lax.fori_loop(0, rows, attend_row, 0, unroll=unroll)

    attn = jnp.concatenate(
        [
            jnp.concatenate([attn_rows[:, s * per_group + j, :] for j in range(per_group)], axis=1)
            for s in range(steps)
        ],
        axis=0,
    ).astype(jnp.bfloat16)

    def project(t, carry):
        weight_copy(t).wait()

        def piece(u, inner):
            at = pl.ds(pl.multiple_of(u * cut, cut), cut)
            product = jnp.dot(attn, weight_buf[t, :, at], preferred_element_type=jnp.float32)
            out[t, :, at] = product.astype(out.dtype)
            return inner

        return lax.fori_loop(0, columns // cut, piece, carry)

    lax.fori_loop(0, parts, project, 0)


def attend_project(
    cut, unroll, parts, block_table, lengths, queries, new_keys, new_values, key_pool, value_pool, out_weight
):
    steps, rows, width = queries.shape
    pool, page, head = key_pool.shape[1:]
    columns = out_weight.shape[1] // parts
    heads = width // head
    return pl.pallas_call(
        functools.partial(attend_kernel, cut, unroll),
        out_shape=jax.ShapeDtypeStruct((parts, steps * rows, columns), jnp.bfloat16),
        in_specs=[SMEM, SMEM, VMEM, VMEM, VMEM, ANY, ANY, ANY],
        out_specs=VMEM,
        scratch_shapes=[
            pltpu.VMEM((pool, page, head), key_pool.dtype),
            pltpu.VMEM((pool, page, head), value_pool.dtype),
            pltpu.VMEM((parts, width, columns), out_weight.dtype),
            pltpu.VMEM((rows, steps * heads, head), jnp.float32),
            pltpu.VMEM((rows, steps * heads, head), jnp.float32),
            pltpu.VMEM((steps, rows, head), jnp.float32),
            pltpu.VMEM((steps, rows, head), jnp.float32),
            pltpu.SemaphoreType.DMA((2 + parts,)),
        ],
        compiler_params=pltpu.CompilerParams(vmem_limit_bytes=24 << 20),
        cost_estimate=pl.CostEstimate(
            flops=160_000_000, bytes_accessed=11 << 20, transcendentals=32768
        ),
    )(block_table, lengths, queries, new_keys, new_values, key_pool, value_pool, out_weight)


def diagonal(rows):
    at = [lax.broadcasted_iota(jnp.int32, (rows, 128), axis) for axis in range(2)]
    return at[0] == at[1]


def sum_kernel(parts, residual, summed, squares):
    def add(t, total):
        return total + parts[t].astype(jnp.float32)

    total = lax.fori_loop(0, parts.shape[0], add, residual[...].astype(jnp.float32))
    summed[...] = total
    square = jnp.sum(total * total, axis=1, keepdims=True)
    square = jnp.sum(jnp.where(diagonal(total.shape[0]), square, 0.0), axis=0, keepdims=True)
    for t in range(squares.shape[0]):
        squares[t] = square


def add_parts(parts, residual):
    count, rows, columns = parts.shape
    return pl.pallas_call(
        sum_kernel,
        out_shape=(
            jax.ShapeDtypeStruct((rows, columns), jnp.float32),
            jax.ShapeDtypeStruct((count, 1, 128), jnp.float32),
        ),
        in_specs=[VMEM, VMEM],
        out_specs=(VMEM, VMEM),
        cost_estimate=pl.CostEstimate(flops=200_000, bytes_accessed=700_000, transcendentals=0),
    )(parts, residual)


def finish_kernel(
    features, squares, summed, gain_in, moved, mixed_out, keys_out, values_out,
    gain, buf, mixed, gain_sem, page_sems, out_sems,
):
    pieces = page_sems.shape[0]
    per_array = pieces // 2
    size = buf.shape[1] // per_array

    def at(k):
        return (pl.ds(k // per_array, 1), pl.ds(k % per_array * size, size))

    arrive = [
        pltpu.make_async_copy(moved.at[at(k)], buf.at[at(k)], page_sems.at[k]) for k in range(pieces)
    ]
    small = [pltpu.make_async_copy(gain_in, gain, gain_sem)]
    leave = [
        pltpu.make_async_copy(
            buf.at[at(k)],
            (keys_out, values_out)[k // per_array].at[:, pl.ds(k % per_array * size, size)],
            out_sems.at[k],
        )
        for k in range(pieces)
    ]
    leave.append(pltpu.make_async_copy(mixed, mixed_out, out_sems.at[pieces]))
    for copy in arrive + small:
        copy.start()
    for k in range(pieces):
        arrive[k].wait()
        leave[k].start()
    for copy in small:
        copy.wait()
    total = squares[0]
    for t in range(1, squares.shape[0]):
        total = total + squares[t]
    total = jnp.where(diagonal(summed.shape[0]), total, 0.0)
    factor = lax.rsqrt(jnp.sum(total, axis=1, keepdims=True) / features + 1e-05)
    scaled = (summed[...] * factor * gain[...]).astype(mixed.dtype)
    mixed[...] = scaled
    leave[pieces].start()
    for copy in leave:
        copy.wait()


def finish(squares, summed, gain, moved, steps, features):
    rows, columns = summed.shape
    pieces = 4
    gain = gain.reshape(1, columns)
    shape = jax.ShapeDtypeStruct((1,) + moved.shape[1:], moved.dtype)
    mixed, moved_keys, moved_values = pl.pallas_call(
        functools.partial(finish_kernel, features),
        out_shape=(jax.ShapeDtypeStruct(summed.shape, jnp.bfloat16), shape, shape),
        in_specs=[VMEM, VMEM, ANY, ANY],
        out_specs=(ANY, ANY, ANY),
        scratch_shapes=[
            pltpu.VMEM(gain.shape, gain.dtype),
            pltpu.VMEM(moved.shape, moved.dtype),
            pltpu.VMEM(summed.shape, jnp.bfloat16),
            pltpu.SemaphoreType.DMA,
            pltpu.SemaphoreType.DMA((pieces,)),
            pltpu.SemaphoreType.DMA((pieces + 1,)),
        ],
        cost_estimate=pl.CostEstimate(flops=50_000, bytes_accessed=1 << 22, transcendentals=16),
    )(squares, summed, gain, moved)
    return (mixed.reshape(steps, rows // steps, columns), moved_keys, moved_values)


def layer(short, residual, *attended):
    cut, unroll = (1024, 4) if short else (512, 1)
    partial_sums = attend_project(cut, unroll, lax.axis_size("tp"), *attended)
    parts = lax.all_to_all(partial_sums, "tp", 0, 0, tiled=True)
    summed, squares = add_parts(parts, residual)
    return (lax.all_to_all(squares, "tp", 0, 0, tiled=True), summed)


def shards(
    hidden_in,
    queries,
    new_keys,
    new_values,
    key_pool,
    value_pool,
    out_weight,
    gain,
    lengths,
    block_table,
    mig_ids,
    partner,
):
    count = lax.axis_size("replica")
    offset = jnp.bitwise_xor(partner[0], lax.axis_index("replica"))
    page_table = block_table.T
    moving, residual = gather_pages(
        page_table,
        mig_ids,
        key_pool,
        value_pool,
        hidden_in.reshape(-1, hidden_in.shape[2]),
        gain.shape[0],
    )

    def branch(distance):
        route = [(i, i ^ distance) for i in range(count)]
        short = distance in SHORT

        def body(moving, *rest):
            moved = lax.ppermute(moving, "replica", route)
            return (*layer(short, *rest), moved)

        return body

    squares, summed, moved = lax.switch(
        offset - 1,
        [branch(distance) for distance in range(1, count)],
        moving, residual,
        page_table, lengths, queries, new_keys, new_values, key_pool, value_pool, out_weight,
    )
    return finish(squares, summed, gain, moved, hidden_in.shape[0], hidden_in.shape[2])


def solution(mesh):
    placed = (
        P(None, "replica", None),
        P(None, "replica", "tp"),
        P(None, "replica", "tp"),
        P(None, "replica", "tp"),
        P("tp", "replica", None, None),
        P("tp", "replica", None, None),
        P("tp", None),
        P("tp"),
        P("replica", None),
        P("replica", None),
        P("replica", None),
        P("replica"),
    )
    return jax.shard_map(
        shards,
        mesh=mesh,
        in_specs=placed,
        out_specs=(
            P(None, "replica", "tp"),
            P("tp", "replica", None, None),
            P("tp", "replica", None, None),
        ),
        check_vma=False,
    )
```

```python
import functools

import jax
import jax.numpy as jnp
from jax import lax
from jax.experimental import pallas as pl
from jax.experimental.pallas import tpu as pltpu
from jax.sharding import PartitionSpec as P

SHORT = (1, 4, 5)
VMEM = pl.BlockSpec(memory_space=pltpu.VMEM)
SMEM = pl.BlockSpec(memory_space=pltpu.SMEM)
ANY = pl.BlockSpec(memory_space=pl.ANY)
HBM = pl.BlockSpec(memory_space=pltpu.HBM)


def gather_kernel(
    table_in, ids_in, keys, values, hidden, out, residual, table, ids, scalar_sems, sems, row_sem
):
    count, pages = (ids.shape[1], table.shape[0])
    scalars = [
        pltpu.make_async_copy(table_in, table, scalar_sems.at[0]),
        pltpu.make_async_copy(ids_in, ids, scalar_sems.at[1]),
    ]
    columns = residual.shape[1]
    own = pl.ds(pl.multiple_of(lax.axis_index("tp") * columns, columns), columns)
    rows = pltpu.make_async_copy(hidden.at[:, own], residual, row_sem)
    for copy in scalars:
        copy.start()
    for copy in scalars:
        copy.wait()
    for m in range(count):
        row = ids[0, m]
        for i in range(pages):
            source = pl.ds(table[i, row], 1)
            target = pl.ds(m * pages + i, 1)
            for k, pool in enumerate((keys, values)):
                pltpu.make_async_copy(
                    pool.at[:, source], out.at[pl.ds(k, 1), target], sems.at[k]
                ).start()
    rows.start()
    for k, pool in enumerate((keys, values)):
        pltpu.make_async_copy(
            pool.at[:, pl.ds(0, count * pages)], out.at[pl.ds(k, 1)], sems.at[k]
        ).wait()
    rows.wait()


def gather_pages(block_table, mig_ids, key_pool, value_pool, hidden, columns):
    moved = mig_ids.shape[1] * block_table.shape[0]
    shape = jax.ShapeDtypeStruct((2, moved) + key_pool.shape[2:], key_pool.dtype)
    return pl.pallas_call(
        gather_kernel,
        out_shape=(shape, jax.ShapeDtypeStruct((hidden.shape[0], columns), hidden.dtype)),
        in_specs=[HBM, HBM, ANY, ANY, ANY],
        out_specs=(ANY, ANY),
        scratch_shapes=[
            pltpu.SMEM(block_table.shape, block_table.dtype),
            pltpu.SMEM(mig_ids.shape, mig_ids.dtype),
            pltpu.SemaphoreType.DMA((2,)),
            pltpu.SemaphoreType.DMA((2,)),
            pltpu.SemaphoreType.DMA,
        ],
        cost_estimate=pl.CostEstimate(flops=0, bytes_accessed=1 << 22, transcendentals=0),
    )(block_table, mig_ids, key_pool, value_pool, hidden)


def attend_kernel(
    cut, unroll, table, lengths, queries, new_keys, new_values, keys, values, weight,
    out, key_buf, value_buf, weight_buf, query_rows, attn_rows, fresh_k, fresh_v, sems,
):
    steps, rows, width = queries.shape
    page, head = key_buf.shape[1:]
    per_group = width // head
    pages = table.shape[0]
    parts, columns = (weight_buf.shape[0], weight_buf.shape[2])

    def weight_copy(t):
        start = pl.multiple_of(t * columns, columns)
        return pltpu.make_async_copy(
            weight.at[:, pl.ds(start, columns)], weight_buf.at[t], sems.at[2 + t]
        )

    key_copy = pltpu.make_async_copy(keys.at[0], key_buf, sems.at[0])
    value_copy = pltpu.make_async_copy(values.at[0], value_buf, sems.at[1])
    key_copy.start()
    value_copy.start()
    def start_weight(t, carry):
        weight_copy(t).start()
        return carry

    lax.fori_loop(0, parts, start_weight, 0)

    for s in range(steps):
        both = queries[s].astype(jnp.float32)
        for j in range(per_group):
            query_rows[:, s * per_group + j, :] = both[:, j * head : (j + 1) * head]
        fresh_k[s] = new_keys[s].astype(jnp.float32)
        fresh_v[s] = new_values[s].astype(jnp.float32)
    scale = 1.0 / jnp.sqrt(jnp.float32(head))
    count = steps * per_group
    step_of = lax.broadcasted_iota(jnp.int32, (count, 1), 0) // per_group
    position = lax.broadcasted_iota(jnp.int32, (count, pages * page), 1)

    key_copy.wait()
    value_copy.wait()

    def attend_row(b, carry):
        query = query_rows[b]
        cached_k = jnp.concatenate([key_buf[table[i, b]] for i in range(pages)], axis=0)
        scores = lax.dot_general(
            query.astype(jnp.bfloat16),
            cached_k,
            (((1,), (1,)), ((), ())),
            preferred_element_type=jnp.float32,
        )
        scores = jnp.where(position < lengths[0, b], scores * scale, -jnp.inf)
        largest = jnp.max(scores, axis=1, keepdims=True)
        fresh = []
        for s in range(steps):
            one = jnp.sum(query * fresh_k[s, pl.ds(b, 1)], axis=1, keepdims=True) * scale
            one = jnp.where(step_of >= s, one, -jnp.inf)
            largest = jnp.maximum(largest, one)
            fresh.append(one)
        raised = jnp.exp(scores - largest)
        fresh = [jnp.exp(one - largest) for one in fresh]
        total = jnp.sum(raised, axis=1, keepdims=True)
        for one in fresh:
            total = total + one
        cached_v = jnp.concatenate([value_buf[table[i, b]] for i in range(pages)], axis=0)
        result = jnp.dot(
            (raised / total).astype(jnp.bfloat16), cached_v, preferred_element_type=jnp.float32
        )
        for s in range(steps):
            weight = (fresh[s] / total).astype(jnp.bfloat16).astype(jnp.float32)
            result = result + weight * fresh_v[s, pl.ds(b, 1)]
        attn_rows[b] = result
        return carry

    lax.fori_loop(0, rows, attend_row, 0, unroll=unroll)

    attn = jnp.concatenate(
        [
            jnp.concatenate([attn_rows[:, s * per_group + j, :] for j in range(per_group)], axis=1)
            for s in range(steps)
        ],
        axis=0,
    ).astype(jnp.bfloat16)

    def project(t, carry):
        weight_copy(t).wait()

        def piece(u, inner):
            at = pl.ds(pl.multiple_of(u * cut, cut), cut)
            product = jnp.dot(attn, weight_buf[t, :, at], preferred_element_type=jnp.float32)
            out[t, :, at] = product.astype(out.dtype)
            return inner

        return lax.fori_loop(0, columns // cut, piece, carry)

    lax.fori_loop(0, parts, project, 0)


def attend_project(
    cut, unroll, parts, block_table, lengths, queries, new_keys, new_values, key_pool, value_pool, out_weight
):
    steps, rows, width = queries.shape
    pool, page, head = key_pool.shape[1:]
    columns = out_weight.shape[1] // parts
    heads = width // head
    return pl.pallas_call(
        functools.partial(attend_kernel, cut, unroll),
        out_shape=jax.ShapeDtypeStruct((parts, steps * rows, columns), jnp.bfloat16),
        in_specs=[SMEM, SMEM, VMEM, VMEM, VMEM, ANY, ANY, ANY],
        out_specs=VMEM,
        scratch_shapes=[
            pltpu.VMEM((pool, page, head), key_pool.dtype),
            pltpu.VMEM((pool, page, head), value_pool.dtype),
            pltpu.VMEM((parts, width, columns), out_weight.dtype),
            pltpu.VMEM((rows, steps * heads, head), jnp.float32),
            pltpu.VMEM((rows, steps * heads, head), jnp.float32),
            pltpu.VMEM((steps, rows, head), jnp.float32),
            pltpu.VMEM((steps, rows, head), jnp.float32),
            pltpu.SemaphoreType.DMA((2 + parts,)),
        ],
        compiler_params=pltpu.CompilerParams(vmem_limit_bytes=24 << 20),
        cost_estimate=pl.CostEstimate(
            flops=160_000_000, bytes_accessed=11 << 20, transcendentals=32768
        ),
    )(block_table, lengths, queries, new_keys, new_values, key_pool, value_pool, out_weight)


def diagonal(rows):
    at = [lax.broadcasted_iota(jnp.int32, (rows, 128), axis) for axis in range(2)]
    return at[0] == at[1]


def sum_kernel(parts, residual, summed, squares):
    def add(t, total):
        return total + parts[t].astype(jnp.float32)

    total = lax.fori_loop(0, parts.shape[0], add, residual[...].astype(jnp.float32))
    summed[...] = total
    square = jnp.sum(total * total, axis=1, keepdims=True)
    square = jnp.sum(jnp.where(diagonal(total.shape[0]), square, 0.0), axis=0, keepdims=True)
    for t in range(squares.shape[0]):
        squares[t] = square


def add_parts(parts, residual):
    count, rows, columns = parts.shape
    return pl.pallas_call(
        sum_kernel,
        out_shape=(
            jax.ShapeDtypeStruct((rows, columns), jnp.float32),
            jax.ShapeDtypeStruct((count, 1, 128), jnp.float32),
        ),
        in_specs=[VMEM, VMEM],
        out_specs=(VMEM, VMEM),
        cost_estimate=pl.CostEstimate(flops=200_000, bytes_accessed=700_000, transcendentals=0),
    )(parts, residual)


def finish_kernel(
    features, squares, summed, gain_in, moved, mixed_out, keys_out, values_out,
    gain, buf, mixed, gain_sem, page_sems, out_sems,
):
    pieces = page_sems.shape[0]
    per_array = pieces // 2
    size = buf.shape[1] // per_array

    def at(k):
        return (pl.ds(k // per_array, 1), pl.ds(k % per_array * size, size))

    arrive = [
        pltpu.make_async_copy(moved.at[at(k)], buf.at[at(k)], page_sems.at[k]) for k in range(pieces)
    ]
    small = [pltpu.make_async_copy(gain_in, gain, gain_sem)]
    leave = [
        pltpu.make_async_copy(
            buf.at[at(k)],
            (keys_out, values_out)[k // per_array].at[:, pl.ds(k % per_array * size, size)],
            out_sems.at[k],
        )
        for k in range(pieces)
    ]
    leave.append(pltpu.make_async_copy(mixed, mixed_out, out_sems.at[pieces]))
    for copy in arrive + small:
        copy.start()
    for k in range(pieces):
        arrive[k].wait()
        leave[k].start()
    for copy in small:
        copy.wait()
    total = squares[0]
    for t in range(1, squares.shape[0]):
        total = total + squares[t]
    total = jnp.where(diagonal(summed.shape[0]), total, 0.0)
    factor = lax.rsqrt(jnp.sum(total, axis=1, keepdims=True) / features + 1e-05)
    scaled = (summed[...] * factor * gain[...]).astype(mixed.dtype)
    mixed[...] = scaled
    leave[pieces].start()
    for copy in leave:
        copy.wait()


def finish(squares, summed, gain, moved, steps, features):
    rows, columns = summed.shape
    pieces = 4
    gain = gain.reshape(1, columns)
    shape = jax.ShapeDtypeStruct((1,) + moved.shape[1:], moved.dtype)
    mixed, moved_keys, moved_values = pl.pallas_call(
        functools.partial(finish_kernel, features),
        out_shape=(jax.ShapeDtypeStruct(summed.shape, jnp.bfloat16), shape, shape),
        in_specs=[VMEM, VMEM, ANY, ANY],
        out_specs=(ANY, ANY, ANY),
        scratch_shapes=[
            pltpu.VMEM(gain.shape, gain.dtype),
            pltpu.VMEM(moved.shape, moved.dtype),
            pltpu.VMEM(summed.shape, jnp.bfloat16),
            pltpu.SemaphoreType.DMA,
            pltpu.SemaphoreType.DMA((pieces,)),
            pltpu.SemaphoreType.DMA((pieces + 1,)),
        ],
        cost_estimate=pl.CostEstimate(flops=50_000, bytes_accessed=1 << 22, transcendentals=16),
    )(squares, summed, gain, moved)
    return (mixed.reshape(steps, rows // steps, columns), moved_keys, moved_values)


def layer(short, residual, *attended):
    cut, unroll = (1024, 4) if short else (512, 1)
    partial_sums = attend_project(cut, unroll, lax.axis_size("tp"), *attended)
    parts = lax.all_to_all(partial_sums, "tp", 0, 0, tiled=True)
    summed, squares = add_parts(parts, residual)
    return (lax.all_to_all(squares, "tp", 0, 0, tiled=True), summed)


def shards(
    hidden_in,
    queries,
    new_keys,
    new_values,
    key_pool,
    value_pool,
    out_weight,
    gain,
    lengths,
    block_table,
    mig_ids,
    partner,
):
    count = lax.axis_size("replica")
    offset = jnp.bitwise_xor(partner[0], lax.axis_index("replica"))
    page_table = block_table.T
    moving, residual = gather_pages(
        page_table,
        mig_ids,
        key_pool,
        value_pool,
        hidden_in.reshape(-1, hidden_in.shape[2]),
        gain.shape[0],
    )

    def branch(distance):
        route = [(i, i ^ distance) for i in range(count)]
        short = distance in SHORT

        def body(moving, *rest):
            moved = lax.ppermute(moving, "replica", route)
            return (*layer(short, *rest), moved)

        return body

    squares, summed, moved = lax.switch(
        offset - 1,
        [branch(distance) for distance in range(1, count)],
        moving, residual,
        page_table, lengths, queries, new_keys, new_values, key_pool, value_pool, out_weight,
    )
    return finish(squares, summed, gain, moved, hidden_in.shape[0], hidden_in.shape[2])


def solution(mesh):
    placed = (
        P(None, "replica", None),
        P(None, "replica", "tp"),
        P(None, "replica", "tp"),
        P(None, "replica", "tp"),
        P("tp", "replica", None, None),
        P("tp", "replica", None, None),
        P("tp", None),
        P("tp"),
        P("replica", None),
        P("replica", None),
        P("replica", None),
        P("replica"),
    )
    return jax.shard_map(
        shards,
        mesh=mesh,
        in_specs=placed,
        out_specs=(
            P(None, "replica", "tp"),
            P("tp", "replica", None, None),
            P("tp", "replica", None, None),
        ),
        check_vma=False,
    )
```
